32 devices in a mesh: expert: 4 (over y, x), fsdp: 8 (over z, core).
Axes of the slice: x: 2, y: 2, z: 4, core: 2. Of those that a mesh axis runs over, the one named last changes fastest.
Arguments:
- tokens: bfloat16 [4608, 2048], P(('expert', 'fsdp')), may hold values from -6 to 6
- expert_ids: int32 [4608, 6], P(('expert', 'fsdp')), may hold values from 0 to 15, as said below
- combine: float32 [4608, 6], P(('expert', 'fsdp')), may hold values from 0.05 to 1
- gate_weight: bfloat16 [16, 1408, 2048], P('expert', 'fsdp'), may hold values from -0.125 to 0.125
- up_weight: bfloat16 [16, 1408, 2048], P('expert', 'fsdp'), may hold values from -0.125 to 0.125
- down_weight: bfloat16 [16, 1408, 2048], P('expert', 'fsdp'), may hold values from -0.15625 to 0.15625
Outputs:
- mixed: bfloat16 [4608, 2048], P(('expert', 'fsdp'))
The draws below stay inside these ranges and needn't reach their ends.
Inputs may be any that keep to these rules, and one draw needn't show every extreme that they name: `expert_ids`: each row names 6 different experts. Within the 144 rows of each device no expert is named more than 72 times, and one and the same expert is named exactly 72 times by the rows of every device.
All inputs are finite; a program needn't handle non-finite values.
Results may differ from the reference program's by a relative error of at most 0.0058.
Values may be sent and summed in bfloat16 or wider, within the bound.
No kernel may reach another device: no remote copies, remote signals or barrier semaphores. Data moves between devices by JAX's collectives and lax.ppermute only.
A program may use at most 128 MiB of HBM per device.

```python
import math
import jax
import jax.numpy as jnp
from jax import lax

D = 2048
FF = 1408
EXPERTS = 16
TOP = 6
TOK_DEV = 144
CAP = 72
TOKENS = 4608


def draw_expert_ids(key, part):
    block_count = TOKENS // TOK_DEV
    hot_key, rest_key = jax.random.split(jax.random.fold_in(key, 17))
    hot_expert = jax.random.randint(hot_key, (), 0, EXPERTS)
    column = jnp.arange(TOP, dtype=jnp.int32)

    def one_block(block_key):
        first_key, second_key, third_key, fourth_key = jax.random.split(block_key, 4)
        token_rank = jax.random.permutation(first_key, TOK_DEV)
        is_hot = token_rank < CAP
        spread = jax.random.permutation(second_key, TOK_DEV)
        offset = spread * (EXPERTS - 1) // TOK_DEV
        shuffle = jax.random.permutation(third_key, EXPERTS - 1)
        rotation = jax.random.randint(fourth_key, (TOK_DEV,), 0, TOP)
        window_pos = jnp.where(is_hot[:, None], column[None, :] - 1, column[None, :])
        other_index = shuffle[(offset[:, None] + jnp.maximum(window_pos, 0)) % (EXPERTS - 1)]
        other_expert = (hot_expert + 1 + other_index) % EXPERTS
        row_ids = jnp.where(window_pos < 0, hot_expert, other_expert)
        rotated = (column[None, :] + rotation[:, None]) % TOP
        return jnp.take_along_axis(row_ids, rotated, axis=1)
    block_keys = jax.random.split(rest_key, block_count)
    return jax.vmap(one_block)(block_keys).reshape(TOKENS, TOP).astype(jnp.int32)


def levels(key, dims, pieces, least, largest):
    loudness, own = 1.0, jax.random.fold_in(key, 6)
    for dim, blocks in pieces:
        draws = jnp.exp(jax.random.uniform(jax.random.fold_in(own, dim), (blocks,), jnp.float32, least / len(pieces), largest / len(pieces)))
        loudness = loudness * jnp.repeat(draws, dims[dim] // blocks).reshape([-1 if axis == dim else 1 for axis in range(len(dims))])
    return loudness


def normal_values(rng, extent, deviation, bound, cuts=(), kind=jnp.bfloat16):
    gain = levels(rng, extent, cuts, -0.22, 0.18) if cuts else 1.0
    entries = jax.random.normal(rng, extent, jnp.float32) * deviation * gain
    return jnp.minimum(jnp.maximum(entries, -bound), bound).astype(kind)


def setup_inputs(seed: int = 0) -> dict:
    streams_of = jax.random.split(jax.random.key(seed), 7)
    tokens = normal_values(streams_of[0], (TOKENS, D), 1.0, 6.0, ((0, 32),))
    expert_ids = draw_expert_ids(jax.random.fold_in(streams_of[6], 71), 0)
    combine = jnp.clip(jnp.exp(math.log(1.0) - 2.9957323 * jax.random.uniform(streams_of[2], (TOKENS, TOP), jnp.float32) ** levels(streams_of[2], (TOKENS, TOP), ((0, 32),), -0.2, 0.2)), 0.05, 1.0)
    gate_weight = normal_values(streams_of[3], (EXPERTS, FF, D), D ** -0.5, 0.125, ((0, 4), (1, 8)))
    up_weight = normal_values(streams_of[4], (EXPERTS, FF, D), D ** -0.5, 0.125, ((0, 4), (1, 8)))
    down_weight = normal_values(streams_of[5], (EXPERTS, FF, D), FF ** -0.5, 0.15625, ((0, 4), (1, 8)))
    return {"tokens": tokens, "expert_ids": expert_ids, "combine": combine, "gate_weight": gate_weight, "up_weight": up_weight, "down_weight": down_weight}


def reference(tokens, expert_ids, combine, gate_weight, up_weight, down_weight):
    limit_rows = (TOKENS // TOK_DEV) * CAP

    def one_expert(running, expert_index):
        chosen = expert_ids == expert_index
        weight = jnp.sum(jnp.where(chosen, combine, jnp.zeros_like(combine)), axis=1)
        named = jnp.any(chosen, axis=1)
        picked = jnp.argsort(jnp.where(named, 0, 1).astype(jnp.int32), stable=True)[:limit_rows].astype(jnp.int32)
        chosen_rows = tokens[picked]
        gate_pre = jnp.dot(chosen_rows, gate_weight[expert_index].T, preferred_element_type=jnp.float32)
        up_pre = jnp.dot(chosen_rows, up_weight[expert_index].T, preferred_element_type=jnp.float32)
        hidden = (jax.nn.silu(gate_pre) * up_pre).astype(jnp.bfloat16)
        produced = jnp.dot(hidden, down_weight[expert_index], preferred_element_type=jnp.float32).astype(jnp.bfloat16)
        term = weight[picked][:, None] * produced.astype(jnp.float32)
        return running.at[picked].add(term), None

    running, unused = lax.scan(one_expert, jnp.zeros((TOKENS, D), jnp.float32), jnp.arange(EXPERTS, dtype=jnp.int32))
    return running.astype(jnp.bfloat16)
```

```python
import jax
import jax.numpy as jnp
from jax import lax
from jax.sharding import Mesh, PartitionSpec as P

PLANE = ("e_hi", "e_lo", "line")
AXES = ("e_hi", "e_lo", "line", "core")


def half_hidden(rows, col_weight, gate, up):
    gate_pre = lax.dot_general(
        rows, gate, (((1,), (1,)), ((), ())), preferred_element_type=jnp.float32
    )
    up_pre = lax.dot_general(
        rows, up, (((1,), (1,)), ((), ())), preferred_element_type=jnp.float32
    )
    return (jax.nn.silu(gate_pre) * up_pre * col_weight).astype(jnp.bfloat16)


def per_device(tokens, expert_ids, combine, gate_weight, up_weight, down_weight):
    groups = lax.axis_size("e_hi") * lax.axis_size("e_lo")
    group = lax.axis_index(("e_hi", "e_lo"))
    per_group, units, width = gate_weight.shape
    experts = groups * per_group
    chosen = expert_ids[:, :, None] == jnp.arange(experts, dtype=jnp.int32)[None, None, :]
    dense_weight = jnp.sum(jnp.where(chosen, combine[:, :, None], 0.0), axis=1)

    swap = [(0, 1), (1, 0)]
    flat = [w.reshape(per_group * units, width) for w in (gate_weight, up_weight, down_weight)]
    other = [lax.ppermute(w, "core", swap) for w in flat]

    all_weight = lax.all_gather(dense_weight, PLANE, axis=0, tiled=True)
    rows = lax.all_gather(tokens, PLANE, axis=0, tiled=True)
    mine = lax.dynamic_slice_in_dim(all_weight, group * per_group, per_group, axis=1)
    column = jnp.arange(per_group * units, dtype=jnp.int32)[None, :]
    col_weight = mine[:, per_group - 1 :]
    for i in range(per_group - 2, -1, -1):
        col_weight = jnp.where(column < (i + 1) * units, mine[:, i : i + 1], col_weight)
    hidden = [half_hidden(rows, col_weight, gate, up) for gate, up, _ in (flat, other)]
    down = jnp.concatenate([flat[2], other[2]], axis=0)
    partial = jnp.dot(
        jnp.concatenate(hidden, axis=1), down, preferred_element_type=jnp.float32
    ).astype(jnp.bfloat16)
    return lax.psum_scatter(partial, PLANE, scatter_dimension=0, tiled=True)


def solution(mesh):
    groups, shards = mesh.shape["expert"], mesh.shape["fsdp"]
    split = Mesh(mesh.devices.reshape(groups // 2, 2, shards // 2, 2), AXES)
    whole, expert, shard = P(AXES, None), ("e_hi", "e_lo"), ("line", "core")
    return jax.shard_map(
        per_device,
        mesh=split,
        in_specs=(whole, whole, whole) + (P(expert, shard, None),) * 3,
        out_specs=whole,
        check_vma=False,
    )
```

```python
import functools

import jax
import jax.numpy as jnp
from jax import lax
from jax.experimental import pallas as pl
from jax.experimental.pallas import tpu as pltpu
from jax.sharding import Mesh, PartitionSpec as P

AXES = ("e_hi", "e_lo", "line", "core")
LANES = 128
TILE = 256


def tiles(extent, size=TILE):
    return [(at, min(size, extent - at)) for at in range(0, extent, size)]


def ffn_kernel(ny, nx, cut, experts, per_group, *refs):
    blocks = ny * nx + (ny - 1) * (nx - 1)
    group = refs[0][0]
    inputs, refs = refs[1 : 1 + blocks], refs[1 + blocks :]
    weights, refs = refs[:6], refs[6:]
    send_a, keep_a, send_b, keep_b = refs[:4]
    rows, held, hidden, total, row_sem, weight_sem = refs[4:]
    depth = total.shape[1]
    half = depth // 2
    units = hidden.shape[1]
    tok = rows.shape[0] // (ny * nx)
    count = rows.shape[0]

    row_copies, at, i = [], 0, 0
    for jy in range(ny):
        for jx in range(nx):
            parts = 2 if jy and jx else 1
            for _ in range(parts):
                size = inputs[i].shape[0]
                row_copies.append(
                    pltpu.make_async_copy(inputs[i], rows.at[pl.ds(at, size)], row_sem.at[i])
                )
                at, i = at + size, i + 1
    weight_copies = [
        pltpu.make_async_copy(weights[j], held.at[j], weight_sem.at[j]) for j in range(6)
    ]
    for copy in row_copies + weight_copies:
        copy.start()
    for copy in row_copies:
        copy.wait()

    extra = rows[:, depth:].astype(jnp.float32)
    lane = lax.broadcasted_iota(jnp.int32, extra.shape, 1)
    named = []
    for e in range(per_group):
        own = group * per_group + e
        pick = (lane == own) | (lane == own + experts)
        named.append(jnp.sum(jnp.where(pick, extra, 0.0), axis=1, keepdims=True))

    per_expert = units // per_group
    for h in range(2):
        gate, up, down = held.at[3 * h], held.at[3 * h + 1], held.at[3 * h + 2]
        weight_copies[3 * h].wait()
        weight_copies[3 * h + 1].wait()
        for start, size in tiles(units):
            nt = (((1,), (1,)), ((), ()))
            gate_pre = lax.dot_general(
                rows[:, :depth],
                gate[start : start + size],
                nt,
                preferred_element_type=jnp.float32,
            )
            up_pre = lax.dot_general(
                rows[:, :depth],
                up[start : start + size],
                nt,
                preferred_element_type=jnp.float32,
            )
            column = lax.broadcasted_iota(jnp.int32, (count, size), 1) + start
            scale = jnp.broadcast_to(named[per_group - 1], (count, size))
            for e in range(per_group - 2, -1, -1):
                scale = jnp.where(column < (e + 1) * per_expert, named[e], scale)
            value = gate_pre / (1.0 + jnp.exp(-gate_pre)) * up_pre * scale
            hidden[:, start : start + size] = value.astype(jnp.bfloat16)
        weight_copies[3 * h + 2].wait()
        for start, size in tiles(depth):
            part = jnp.dot(
                hidden[...], down[:, start : start + size], preferred_element_type=jnp.float32
            )
            cols = slice(start, start + size)
            if h == 0:
                total[:, cols] = part
                continue
            part = part + total[:, cols]
            to = slice(start % half, start % half + size)
            for jy in range(ny):
                for jx in range(nx):
                    at = (jy * nx + jx) * tok
                    block = part[at : at + tok]
                    if start < half:
                        there = slice(jx * tok, (jx + 1) * tok)
                        if jy:
                            send_a[jy - 1, there, to] = block.astype(jnp.bfloat16)
                        else:
                            keep_a[there, to] = block
                    else:
                        there = slice(jy * tok, (jy + 1) * tok)
                        if jx:
                            send_b[jx - 1, there, to] = block.astype(jnp.bfloat16)
                        else:
                            keep_b[there, to] = block


def ffn(blocks, weights, group, ny, nx, cut, experts, per_group):
    tok, depth = blocks[0].shape[0], weights[0].shape[1]
    units, half = weights[0].shape[0], depth // 2
    count = ny * nx * tok
    any_spec, vmem = pl.BlockSpec(memory_space=pl.ANY), pl.BlockSpec(memory_space=pltpu.VMEM)
    macs = count * depth * units * 6
    return pl.pallas_call(
        functools.partial(ffn_kernel, ny, nx, cut, experts, per_group),
        in_specs=[pl.BlockSpec(memory_space=pltpu.SMEM)] + [any_spec] * (len(blocks) + 6),
        out_specs=[vmem] * 4,
        out_shape=[
            jax.ShapeDtypeStruct((ny - 1, nx * tok, half), jnp.bfloat16),
            jax.ShapeDtypeStruct((nx * tok, half), jnp.float32),
            jax.ShapeDtypeStruct((nx - 1, ny * tok, half), jnp.bfloat16),
            jax.ShapeDtypeStruct((ny * tok, half), jnp.float32),
        ],
        scratch_shapes=[
            pltpu.VMEM((count, blocks[0].shape[1]), jnp.bfloat16),
            pltpu.VMEM((6, units, depth), jnp.bfloat16),
            pltpu.VMEM((count, units), jnp.bfloat16),
            pltpu.VMEM((count, depth), jnp.float32),
            pltpu.SemaphoreType.DMA((len(blocks),)),
            pltpu.SemaphoreType.DMA((6,)),
        ],
        compiler_params=pltpu.CompilerParams(vmem_limit_bytes=56 * 1024 * 1024),
        cost_estimate=pl.CostEstimate(
            flops=2 * macs,
            bytes_accessed=12 * units * depth + 8 * count * depth,
            transcendentals=2 * count * units,
        ),
    )(group, *blocks, *weights)


def shift(value, axis, by):
    n = lax.axis_size(axis)
    return lax.ppermute(value, axis, [(i, (i + by) % n) for i in range(n)])


def ring_step(value):
    n = lax.axis_size("line")
    order = list(range(1, n, 2)) + list(range(0, n, 2))[::-1]
    return lax.ppermute(value, "line", [(order[i], order[(i + 1) % n]) for i in range(n)])


def per_device(tokens, expert_ids, combine, gate_weight, up_weight, down_weight):
    ny, nx, stages = lax.axis_size("e_hi"), lax.axis_size("e_lo"), lax.axis_size("line")
    per_group, units, depth = gate_weight.shape
    experts = ny * nx * per_group
    tok = tokens.shape[0]
    half = depth // 2
    cut = (tok // 2 + 15) // 16 * 16
    group = lax.axis_index(("e_hi", "e_lo")).astype(jnp.int32).reshape(1)

    chosen = expert_ids[:, :, None] == jnp.arange(experts, dtype=jnp.int32)[None, None, :]
    named = jnp.sum(jnp.where(chosen, combine[:, :, None], 0.0), axis=1)
    high = named.astype(jnp.bfloat16)
    rest = (named - high.astype(jnp.float32)).astype(jnp.bfloat16)
    pad = jnp.zeros((tok, LANES * -(-2 * experts // LANES) - 2 * experts), jnp.bfloat16)
    mine = jnp.concatenate([tokens, high, rest, pad], axis=1)

    flat = [w.reshape(per_group * units, depth) for w in (gate_weight, up_weight, down_weight)]
    weights = flat + [shift(w, "core", 1) for w in flat]

    slot = [mine]
    for _ in range(stages - 1):
        slot.append(ring_step(slot[-1]))

    def gathered(block):
        along_x = [block] + [shift(block, "e_lo", j) for j in range(1, nx)]
        along_y = [block] + [shift(block, "e_hi", j) for j in range(1, ny)]
        out = []
        for jy in range(ny):
            for jx in range(nx):
                if jy and jx:
                    out.append(shift(along_x[jx][:cut], "e_hi", jy))
                    out.append(shift(along_y[jy][cut:], "e_lo", jx))
                else:
                    out.append(along_x[jx] if jx else along_y[jy])
        return out

    def add(*terms):
        return sum(t.astype(jnp.float32) for t in terms)

    def first_sums(k):
        send_a, keep_a, send_b, keep_b = ffn(
            gathered(slot[k]), weights, group, ny, nx, cut, experts, per_group
        )
        got_a = [shift(send_a[j - 1], "e_hi", -j) for j in range(1, ny)]
        got_b = [shift(send_b[j - 1], "e_lo", -j) for j in range(1, nx)]
        return [keep_a] + got_a, [keep_b] + got_b

    sums = [first_sums(k) for k in range(stages)]
    carry_a, carry_b = [], []
    for k in list(range(1, stages)):
        carry_a = [ring_step(add(*sums[k][0], *carry_a).astype(jnp.bfloat16))]
        carry_b = [ring_step(add(*sums[k][1], *carry_b).astype(jnp.bfloat16))]
    total_a = add(*sums[0][0], *carry_a).reshape(nx, tok, half)
    total_b = add(*sums[0][1], *carry_b).reshape(ny, tok, half)
    last_a = [shift(total_a[j].astype(jnp.bfloat16), "e_lo", -j) for j in range(1, nx)]
    last_b = [shift(total_b[j].astype(jnp.bfloat16), "e_hi", -j) for j in range(1, ny)]
    return jnp.concatenate(
        [
            add(total_a[0], *last_a).astype(jnp.bfloat16),
            add(total_b[0], *last_b).astype(jnp.bfloat16),
        ],
        axis=1,
    )


def solution(mesh):
    groups, shards = mesh.shape["expert"], mesh.shape["fsdp"]
    split = Mesh(mesh.devices.reshape(groups // 2, 2, shards // 2, 2), AXES)
    whole, expert, shard = P(AXES, None), ("e_hi", "e_lo"), ("line", "core")
    return jax.shard_map(
        per_device,
        mesh=split,
        in_specs=(whole, whole, whole) + (P(expert, shard, None),) * 3,
        out_specs=whole,
        check_vma=False,
    )
```

```python
import functools

import jax
import jax.numpy as jnp
from jax import lax
from jax.experimental import pallas as pl
from jax.experimental.pallas import tpu as pltpu
from jax.sharding import Mesh, PartitionSpec as P

AXES = ("e_hi", "e_lo", "line", "core")
LANES = 128
TILE = 256


def tiles(extent, size=TILE):
    return [(at, min(size, extent - at)) for at in range(0, extent, size)]


def ffn_kernel(ny, nx, experts, per_group, *refs):
    place, gathered = refs[:2]
    weights, refs = refs[2:8], refs[8:]
    send_a, keep_a, send_b, keep_b = refs[:4]
    rows, gates, ups, downs, hidden, row_sem, weight_sem = refs[4:]
    count, depth = rows.shape[0], downs.shape[1]
    half = depth // 2
    units = hidden.shape[1] // 2
    tok = count // (ny * nx)
    group, my_y, my_x = place[0], place[1], place[2]

    row_copies = []
    for jy in range(ny):
        for jx in range(nx):
            block = lax.rem(my_y + ny - jy, ny) * nx + lax.rem(my_x + nx - jx, nx)
            at = jy * nx + jx
            row_copies.append(
                pltpu.make_async_copy(
                    gathered.at[pl.ds(pl.multiple_of(block * tok, tok), tok)],
                    rows.at[pl.ds(at * tok, tok)],
                    row_sem.at[at],
                )
            )
    targets = [gates.at[0], ups.at[0], gates.at[1], ups.at[1]]
    targets += [downs.at[pl.ds(0, units)], downs.at[pl.ds(units, units)]]
    weight_copies = [
        pltpu.make_async_copy(weights[j], targets[j], weight_sem.at[j]) for j in range(6)
    ]
    for copy in row_copies + weight_copies:
        copy.start()
    for copy in row_copies:
        copy.wait()

    extra = rows[:, depth:].astype(jnp.float32)
    lane = lax.broadcasted_iota(jnp.int32, extra.shape, 1)
    named = []
    for e in range(per_group):
        own = group * per_group + e
        pick = (lane == own) | (lane == own + experts)
        named.append(0.5 * jnp.sum(jnp.where(pick, extra, 0.0), axis=1, keepdims=True))

    per_expert = units // per_group
    for h in range(2):
        weight_copies[2 * h].wait()
        weight_copies[2 * h + 1].wait()
        for start, size in tiles(units):
            cols = slice(start, start + size)
            gate_pre = jnp.dot(
                rows[:, :depth], gates[h, :, cols], preferred_element_type=jnp.float32
            )
            up_pre = jnp.dot(
                rows[:, :depth], ups[h, :, cols], preferred_element_type=jnp.float32
            )
            first, last = start // per_expert, (start + size - 1) // per_expert
            column = lax.broadcasted_iota(jnp.int32, (1, size), 1) + start
            scale = named[last]
            for e in range(last - 1, first - 1, -1):
                scale = jnp.where(column < (e + 1) * per_expert, named[e], scale)
            value = gate_pre * (1.0 + jnp.tanh(0.5 * gate_pre)) * (up_pre * scale)
            at = h * units + start
            hidden[:, at : at + size] = value.astype(jnp.bfloat16)
    weight_copies[4].wait()
    weight_copies[5].wait()
    for start, size in tiles(depth):
        part = jnp.dot(
            hidden[...], downs[:, start : start + size], preferred_element_type=jnp.float32
        )
        to = slice(start % half, start % half + size)
        for jy in range(ny):
            for jx in range(nx):
                at = (jy * nx + jx) * tok
                block = part[at : at + tok]
                if start < half:
                    there = slice(jx * tok, (jx + 1) * tok)
                    if jy:
                        send_a[jy - 1, there, to] = block.astype(jnp.bfloat16)
                    else:
                        keep_a[there, to] = block
                else:
                    there = slice(jy * tok, (jy + 1) * tok)
                    if jx:
                        send_b[jx - 1, there, to] = block.astype(jnp.bfloat16)
                    else:
                        keep_b[there, to] = block


def ffn(gathered, weights, place, ny, nx, experts, per_group):
    count, width = gathered.shape
    units, depth = weights[-1].shape
    tok, half = count // (ny * nx), depth // 2
    any_spec, vmem = pl.BlockSpec(memory_space=pl.ANY), pl.BlockSpec(memory_space=pltpu.VMEM)
    macs = count * depth * units * 6
    return pl.pallas_call(
        functools.partial(ffn_kernel, ny, nx, experts, per_group),
        in_specs=[pl.BlockSpec(memory_space=pltpu.SMEM)] + [any_spec] * 7,
        out_specs=[vmem] * 4,
        out_shape=[
            jax.ShapeDtypeStruct((ny - 1, nx * tok, half), jnp.bfloat16),
            jax.ShapeDtypeStruct((nx * tok, half), jnp.float32),
            jax.ShapeDtypeStruct((nx - 1, ny * tok, half), jnp.bfloat16),
            jax.ShapeDtypeStruct((ny * tok, half), jnp.float32),
        ],
        scratch_shapes=[
            pltpu.VMEM((count, width), jnp.bfloat16),
            pltpu.VMEM((2, depth, units), jnp.bfloat16),
            pltpu.VMEM((2, depth, units), jnp.bfloat16),
            pltpu.VMEM((2 * units, depth), jnp.bfloat16),
            pltpu.VMEM((count, 2 * units), jnp.bfloat16),
            pltpu.SemaphoreType.DMA((ny * nx,)),
            pltpu.SemaphoreType.DMA((6,)),
        ],
        compiler_params=pltpu.CompilerParams(vmem_limit_bytes=44 * 1024 * 1024),
        cost_estimate=pl.CostEstimate(
            flops=2 * macs,
            bytes_accessed=12 * units * depth + 8 * count * depth,
            transcendentals=2 * count * units,
        ),
    )(place, gathered, *weights)


def shift(value, axis, by):
    n = lax.axis_size(axis)
    return lax.ppermute(value, axis, [(i, (i + by) % n) for i in range(n)])


def ring_step(value):
    n = lax.axis_size("line")
    order = list(range(1, n, 2)) + list(range(0, n, 2))[::-1]
    return lax.ppermute(value, "line", [(order[i], order[(i + 1) % n]) for i in range(n)])


def per_device(tokens, expert_ids, combine, gate_weight, up_weight, down_weight):
    ny, nx, stages = lax.axis_size("e_hi"), lax.axis_size("e_lo"), lax.axis_size("line")
    per_group, units, depth = gate_weight.shape
    experts = ny * nx * per_group
    tok = tokens.shape[0]
    half = depth // 2
    place = jnp.stack(
        [lax.axis_index(axis) for axis in (("e_hi", "e_lo"), "e_hi", "e_lo")]
    ).astype(jnp.int32)

    chosen = expert_ids[:, :, None] == jnp.arange(experts, dtype=jnp.int32)[None, None, :]
    named = jnp.sum(jnp.where(chosen, combine[:, :, None], 0.0), axis=1)
    high = named.astype(jnp.bfloat16)
    rest = (named - high.astype(jnp.float32)).astype(jnp.bfloat16)
    pad = jnp.zeros((tok, LANES * -(-2 * experts // LANES) - 2 * experts), jnp.bfloat16)
    mine = jnp.concatenate([tokens, high, rest, pad], axis=1)

    gate, up, down = [
        w.reshape(per_group * units, depth) for w in (gate_weight, up_weight, down_weight)
    ]
    own = [gate.T, up.T, down]
    other = [shift(w, "core", 1) for w in own]
    weights = own[:2] + other[:2] + [own[2], other[2]]

    slot = [mine]
    for _ in range(stages - 1):
        slot.append(ring_step(slot[-1]))

    def add(*terms):
        return sum(t.astype(jnp.float32) for t in terms)

    def first_sums(k):
        gathered = lax.all_gather(slot[k], ("e_hi", "e_lo"), axis=0, tiled=True)
        send_a, keep_a, send_b, keep_b = ffn(
            gathered, weights, place, ny, nx, experts, per_group
        )
        got_a = [shift(send_a[j - 1], "e_hi", -j) for j in range(1, ny)]
        got_b = [shift(send_b[j - 1], "e_lo", -j) for j in range(1, nx)]
        return [keep_a] + got_a, [keep_b] + got_b

    sums = [first_sums(k) for k in range(stages)]
    carry_a, carry_b = [], []
    for k in list(range(1, stages)):
        carry_a = [ring_step(add(*sums[k][0], *carry_a).astype(jnp.bfloat16))]
        carry_b = [ring_step(add(*sums[k][1], *carry_b).astype(jnp.bfloat16))]
    total_a = add(*sums[0][0], *carry_a).reshape(nx, tok, half)
    total_b = add(*sums[0][1], *carry_b).reshape(ny, tok, half)
    last_a = [shift(total_a[j].astype(jnp.bfloat16), "e_lo", -j) for j in range(1, nx)]
    last_b = [shift(total_b[j].astype(jnp.bfloat16), "e_hi", -j) for j in range(1, ny)]
    return jnp.concatenate(
        [
            add(total_a[0], *last_a).astype(jnp.bfloat16),
            add(total_b[0], *last_b).astype(jnp.bfloat16),
        ],
        axis=1,
    )


def solution(mesh):
    groups, shards = mesh.shape["expert"], mesh.shape["fsdp"]
    split = Mesh(mesh.devices.reshape(groups // 2, 2, shards // 2, 2), AXES)
    whole, expert, shard = P(AXES, None), ("e_hi", "e_lo"), ("line", "core")
    return jax.shard_map(
        per_device,
        mesh=split,
        in_specs=(whole, whole, whole) + (P(expert, shard, None),) * 3,
        out_specs=whole,
        check_vma=False,
    )
```

```python
import functools

import jax
import jax.numpy as jnp
from jax import lax
from jax.experimental import pallas as pl
from jax.experimental.pallas import tpu as pltpu
from jax.sharding import Mesh, PartitionSpec as P

AXES = ("e_hi", "e_lo", "line", "core")
LANES = 128
TILE = 256


def tiles(extent, size=TILE):
    return [(at, min(size, extent - at)) for at in range(0, extent, size)]


def ffn_kernel(ny, nx, experts, per_group, *refs):
    place, sources, refs = refs[0], refs[1 : 1 + nx + ny], refs[1 + nx + ny :]
    own, other, refs = refs[0], refs[1], refs[2:]
    send_a, keep_a, send_b, keep_b = refs[:4]
    rows, held, hidden, row_sem, weight_sem = refs[4:]
    count, depth = rows.shape[0], held.shape[2]
    half = depth // 2
    units = held.shape[1] // 3
    tok = count // (ny * nx)
    group = place[0]

    row_copies = []
    for jy in range(ny):
        for jx in range(nx):
            at = (jy * nx + jx) * tok
            left, right = sources[jy], sources[ny + jx]
            for source, from_row, to_col in ((left, jx * tok, 0), (right, jy * tok, half)):
                row_copies.append(
                    pltpu.make_async_copy(
                        source.at[pl.ds(from_row, tok)],
                        rows.at[pl.ds(at, tok), pl.ds(to_col, source.shape[1])],
                        row_sem.at[len(row_copies)],
                    )
                )
    chunks = [(0, 2 * units), (2 * units, units)]
    weight_copies = [
        pltpu.make_async_copy(
            source.at[pl.ds(start, size)], held.at[h, pl.ds(start, size)], weight_sem.at[2 * h + c]
        )
        for h, source in enumerate((own, other))
        for c, (start, size) in enumerate(chunks)
    ]
    for copy in row_copies + weight_copies[:1]:
        copy.start()
    for copy in row_copies:
        copy.wait()

    extra = rows[:, depth:].astype(jnp.float32)
    lane = lax.broadcasted_iota(jnp.int32, extra.shape, 1)
    named = []
    for e in range(per_group):
        mine = group * per_group + e
        pick = (lane == mine) | (lane == mine + experts)
        named.append(0.5 * jnp.sum(jnp.where(pick, extra, 0.0), axis=1, keepdims=True))

    per_expert = units // per_group
    nt = (((1,), (1,)), ((), ()))
    for h in range(2):
        weight_copies[2 * h].wait()
        if h == 0:
            weight_copies[2].start()
            weight_copies[1].start()
            weight_copies[3].start()
        for start, size in tiles(units):
            gate_pre = lax.dot_general(
                rows[:, :depth],
                held[h, start : start + size],
                nt,
                preferred_element_type=jnp.float32,
            )
            up_pre = lax.dot_general(
                rows[:, :depth],
                held[h, units + start : units + start + size],
                nt,
                preferred_element_type=jnp.float32,
            )
            first, last = start // per_expert, (start + size - 1) // per_expert
            column = lax.broadcasted_iota(jnp.int32, (1, size), 1) + start
            scale = named[last]
            for e in range(last - 1, first - 1, -1):
                scale = jnp.where(column < (e + 1) * per_expert, named[e], scale)
            value = gate_pre * (1.0 + jnp.tanh(0.5 * gate_pre)) * (up_pre * scale)
            hidden[h, :, start : start + size] = value.astype(jnp.bfloat16)
    weight_copies[1].wait()
    weight_copies[3].wait()
    for start, size in tiles(depth):
        part = sum(
            jnp.dot(
                hidden[h],
                held[h, 2 * units :, start : start + size],
                preferred_element_type=jnp.float32,
            )
            for h in range(2)
        )
        to = slice(start % half, start % half + size)
        for jy in range(ny):
            for jx in range(nx):
                at = (jy * nx + jx) * tok
                block = part[at : at + tok]
                if start < half:
                    there = slice(jx * tok, (jx + 1) * tok)
                    if jy:
                        send_a[jy - 1, there, to] = block.astype(jnp.bfloat16)
                    else:
                        keep_a[there, to] = block
                else:
                    there = slice(jy * tok, (jy + 1) * tok)
                    if jx:
                        send_b[jx - 1, there, to] = block.astype(jnp.bfloat16)
                    else:
                        keep_b[there, to] = block


def ffn(left, right, own, other, place, experts, per_group):
    ny, nx = len(left), len(right)
    tok, half = left[0].shape[0] // nx, left[0].shape[1]
    units, depth = own.shape[0] // 3, own.shape[1]
    count, width = ny * nx * tok, half + right[0].shape[1]
    any_spec, vmem = pl.BlockSpec(memory_space=pl.ANY), pl.BlockSpec(memory_space=pltpu.VMEM)
    macs = count * depth * units * 6
    return pl.pallas_call(
        functools.partial(ffn_kernel, ny, nx, experts, per_group),
        in_specs=[pl.BlockSpec(memory_space=pltpu.SMEM)] + [any_spec] * (ny + nx + 2),
        out_specs=[vmem] * 4,
        out_shape=[
            jax.ShapeDtypeStruct((ny - 1, nx * tok, half), jnp.bfloat16),
            jax.ShapeDtypeStruct((nx * tok, half), jnp.float32),
            jax.ShapeDtypeStruct((nx - 1, ny * tok, half), jnp.bfloat16),
            jax.ShapeDtypeStruct((ny * tok, half), jnp.float32),
        ],
        scratch_shapes=[
            pltpu.VMEM((count, width), jnp.bfloat16),
            pltpu.VMEM((2, 3 * units, depth), jnp.bfloat16),
            pltpu.VMEM((2, count, units), jnp.bfloat16),
            pltpu.SemaphoreType.DMA((2 * ny * nx,)),
            pltpu.SemaphoreType.DMA((4,)),
        ],
        compiler_params=pltpu.CompilerParams(vmem_limit_bytes=36 * 1024 * 1024),
        cost_estimate=pl.CostEstimate(
            flops=2 * macs,
            bytes_accessed=12 * units * depth + 8 * count * depth,
            transcendentals=2 * count * units,
        ),
    )(place, *left, *right, own, other)


def shift(value, axis, by):
    n = lax.axis_size(axis)
    return lax.ppermute(value, axis, [(i, (i + by) % n) for i in range(n)])


def ring_step(value):
    n = lax.axis_size("line")
    order = list(range(1, n, 2)) + list(range(0, n, 2))[::-1]
    return lax.ppermute(value, "line", [(order[i], order[(i + 1) % n]) for i in range(n)])


def after(value, *earlier):
    return lax.optimization_barrier((value, earlier))[0]


def per_device(tokens, expert_ids, combine, gate_weight, up_weight, down_weight):
    ny, nx, stages = lax.axis_size("e_hi"), lax.axis_size("e_lo"), lax.axis_size("line")
    per_group, units, depth = gate_weight.shape
    experts = ny * nx * per_group
    tok = tokens.shape[0]
    half = depth // 2
    group = lax.axis_index(("e_hi", "e_lo")).astype(jnp.int32).reshape(1)

    chosen = expert_ids[:, :, None] == jnp.arange(experts, dtype=jnp.int32)[None, None, :]
    named = jnp.sum(jnp.where(chosen, combine[:, :, None], 0.0), axis=1)
    high = named.astype(jnp.bfloat16)
    rest = (named - high.astype(jnp.float32)).astype(jnp.bfloat16)
    pad = jnp.zeros((tok, LANES * -(-2 * experts // LANES) - 2 * experts), jnp.bfloat16)
    left0 = tokens[:, :half]
    right0 = jnp.concatenate([tokens[:, half:], high, rest, pad], axis=1)

    own = jnp.concatenate(
        [w.reshape(per_group * units, depth) for w in (gate_weight, up_weight, down_weight)]
    )
    other = shift(own, "core", 1)

    def add(*terms):
        return sum(t.astype(jnp.float32) for t in terms)

    left = jnp.concatenate([left0] + [shift(left0, "e_lo", j) for j in range(1, nx)])
    right = jnp.concatenate([right0] + [shift(right0, "e_hi", j) for j in range(1, ny)])

    def start_sums(parts, *earlier):
        send_a, keep_a, send_b, keep_b = parts
        send_a, send_b = after((send_a, send_b), *earlier)
        got_a = [shift(send_a[j - 1], "e_hi", -j) for j in range(1, ny)]
        got_b = [shift(send_b[j - 1], "e_lo", -j) for j in range(1, nx)]
        return [keep_a] + got_a, [keep_b] + got_b

    def finish_sums(terms_a, terms_b):
        sum_a = add(*terms_a).reshape(nx, tok, half)
        sum_b = add(*terms_b).reshape(ny, tok, half)
        last_a = [shift(sum_a[j].astype(jnp.bfloat16), "e_lo", -j) for j in range(1, nx)]
        last_b = [shift(sum_b[j].astype(jnp.bfloat16), "e_hi", -j) for j in range(1, ny)]
        return [sum_a[0]] + last_a, [sum_b[0]] + last_b

    begun, ended, parts = {}, {}, None
    for k in range(stages):
        lefts = [left] + [shift(left, "e_hi", j) for j in range(1, ny)]
        rights = [right] + [shift(right, "e_lo", j) for j in range(1, nx)]
        if k + 1 < stages:
            left, right = ring_step(left), ring_step(right)
        if k:
            begun[k - 1] = start_sums(parts, lefts[1:], rights[1:], ended.get(k - 2))
        parts = ffn(lefts, rights, own, other, group, experts, per_group)
        if k:
            begun[k - 1] = after(begun[k - 1], parts)
            ended[k - 1] = finish_sums(*begun[k - 1])
        if k + 1 < stages:
            left, right = after((left, right), parts, begun.get(k - 1))
    begun[stages - 1] = start_sums(parts, ended[stages - 2])
    ended[stages - 1] = finish_sums(*begun[stages - 1])

    carry = []
    for k in list(range(1, stages)) + [0]:
        a, b = ended[k]
        carried = [c[:, :half] for c in carry], [c[:, half:] for c in carry]
        total = jnp.concatenate([add(*a, *carried[0]), add(*b, *carried[1])], axis=1)
        total = total.astype(jnp.bfloat16)
        carry = [ring_step(total)] if k else [total]
    return carry[0]


def solution(mesh):
    groups, shards = mesh.shape["expert"], mesh.shape["fsdp"]
    split = Mesh(mesh.devices.reshape(groups // 2, 2, shards // 2, 2), AXES)
    whole, expert, shard = P(AXES, None), ("e_hi", "e_lo"), ("line", "core")
    return jax.shard_map(
        per_device,
        mesh=split,
        in_specs=(whole, whole, whole) + (P(expert, shard, None),) * 3,
        out_specs=whole,
        check_vma=False,
    )
```

```python
import functools

import jax
import jax.numpy as jnp
from jax import lax
from jax.experimental import pallas as pl
from jax.experimental.pallas import tpu as pltpu
from jax.sharding import Mesh, PartitionSpec as P

AXES = ("e_hi", "e_lo", "line", "core")
LANES = 128
TILE = 256


def tiles(extent, size=TILE):
    return [(at, min(size, extent - at)) for at in range(0, extent, size)]


def ffn_kernel(ny, nx, experts, per_group, *refs):
    place, refs = refs[0], refs[1:]
    first, refs = refs[0], refs[1:]
    near, refs = refs[: nx + ny - 2], refs[nx + ny - 2 :]
    left, right, refs = refs[: ny - 1], refs[ny - 1 : ny + nx - 2], refs[ny + nx - 2 :]
    weights, refs = refs[:6], refs[6:]
    send_a, keep_a, send_b, keep_b = refs[:4]
    rows, hidden, row_sem = refs[4:]
    count, depth = rows.shape[0], weights[0].shape[1]
    half = depth // 2
    units = weights[0].shape[0]
    tok = count // (ny * nx)
    group = place[0]

    row_copies = []

    def bring(source, from_row, block, low):
        cols = pl.ds(0, half) if low else pl.ds(half, rows.shape[1] - half)
        from_cols = cols if source.shape[1] == rows.shape[1] else pl.ds(0, source.shape[1])
        row_copies.append(
            pltpu.make_async_copy(
                source.at[pl.ds(from_row, tok), from_cols],
                rows.at[pl.ds(block * tok, tok), cols],
                row_sem.at[len(row_copies)],
            )
        )

    for jy in range(ny):
        for jx in range(nx):
            block = jy * nx + jx
            if jy:
                bring(left[jy - 1], jx * tok, block, True)
            else:
                bring(near[jx - 1] if jx else first, 0, block, True)
            if jx:
                bring(right[jx - 1], jy * tok, block, False)
            else:
                bring(near[nx - 1 + jy - 1] if jy else first, 0, block, False)
    for copy in row_copies:
        copy.start()
    for copy in row_copies:
        copy.wait()

    extra = rows[:, depth:].astype(jnp.float32)
    lane = lax.broadcasted_iota(jnp.int32, extra.shape, 1)
    named = []
    for e in range(per_group):
        mine = group * per_group + e
        pick = (lane == mine) | (lane == mine + experts)
        named.append(0.5 * jnp.sum(jnp.where(pick, extra, 0.0), axis=1, keepdims=True))

    per_expert = units // per_group
    nt = (((1,), (1,)), ((), ()))
    for h in range(2):
        gate, up = weights[3 * h], weights[3 * h + 1]
        for start, size in tiles(units):
            gate_pre = lax.dot_general(
                rows[:, :depth],
                gate[start : start + size],
                nt,
                preferred_element_type=jnp.float32,
            )
            up_pre = lax.dot_general(
                rows[:, :depth],
                up[start : start + size],
                nt,
                preferred_element_type=jnp.float32,
            )
            low, high = start // per_expert, (start + size - 1) // per_expert
            column = lax.broadcasted_iota(jnp.int32, (1, size), 1) + start
            scale = named[high]
            for e in range(high - 1, low - 1, -1):
                scale = jnp.where(column < (e + 1) * per_expert, named[e], scale)
            value = gate_pre * (1.0 + jnp.tanh(0.5 * gate_pre)) * (up_pre * scale)
            hidden[h, :, start : start + size] = value.astype(jnp.bfloat16)
    for start, size in tiles(depth):
        part = sum(
            jnp.dot(
                hidden[h],
                weights[3 * h + 2][:, start : start + size],
                preferred_element_type=jnp.float32,
            )
            for h in range(2)
        )
        to = slice(start % half, start % half + size)
        for jy in range(ny):
            for jx in range(nx):
                at = (jy * nx + jx) * tok
                block = part[at : at + tok]
                if start < half:
                    there = slice(jx * tok, (jx + 1) * tok)
                    if jy:
                        send_a[jy - 1, there, to] = block.astype(jnp.bfloat16)
                    else:
                        keep_a[there, to] = block
                else:
                    there = slice(jy * tok, (jy + 1) * tok)
                    if jx:
                        send_b[jx - 1, there, to] = block.astype(jnp.bfloat16)
                    else:
                        keep_b[there, to] = block


def ffn(first, near, left, right, weights, place, experts, per_group):
    ny, nx = len(left) + 1, len(right) + 1
    tok, width = first.shape
    units, depth = weights[0].shape
    half, count = depth // 2, ny * nx * tok
    any_spec, vmem = pl.BlockSpec(memory_space=pl.ANY), pl.BlockSpec(memory_space=pltpu.VMEM)
    sources = [first, *near, *left, *right]
    macs = count * depth * units * 6
    return pl.pallas_call(
        functools.partial(ffn_kernel, ny, nx, experts, per_group),
        in_specs=[pl.BlockSpec(memory_space=pltpu.SMEM)] + [any_spec] * len(sources) + [vmem] * 6,
        out_specs=[vmem] * 4,
        out_shape=[
            jax.ShapeDtypeStruct((ny - 1, nx * tok, half), jnp.bfloat16),
            jax.ShapeDtypeStruct((nx * tok, half), jnp.float32),
            jax.ShapeDtypeStruct((nx - 1, ny * tok, half), jnp.bfloat16),
            jax.ShapeDtypeStruct((ny * tok, half), jnp.float32),
        ],
        scratch_shapes=[
            pltpu.VMEM((count, width), jnp.bfloat16),
            pltpu.VMEM((2, count, units), jnp.bfloat16),
            pltpu.SemaphoreType.DMA((2 * ny * nx,)),
        ],
        compiler_params=pltpu.CompilerParams(vmem_limit_bytes=26 * 1024 * 1024),
        cost_estimate=pl.CostEstimate(
            flops=2 * macs,
            bytes_accessed=8 * count * depth,
            transcendentals=2 * count * units,
        ),
    )(place, *sources, *weights)


def shift(value, axis, by):
    n = lax.axis_size(axis)
    return lax.ppermute(value, axis, [(i, (i + by) % n) for i in range(n)])


def ring_step(value):
    n = lax.axis_size("line")
    order = list(range(1, n, 2)) + list(range(0, n, 2))[::-1]
    return lax.ppermute(value, "line", [(order[i], order[(i + 1) % n]) for i in range(n)])


def after(value, *earlier):
    return lax.optimization_barrier((value, earlier))[0]


def per_device(tokens, expert_ids, combine, gate_weight, up_weight, down_weight):
    ny, nx, stages = lax.axis_size("e_hi"), lax.axis_size("e_lo"), lax.axis_size("line")
    per_group, units, depth = gate_weight.shape
    experts = ny * nx * per_group
    tok = tokens.shape[0]
    half = depth // 2
    group = lax.axis_index(("e_hi", "e_lo")).astype(jnp.int32).reshape(1)

    chosen = expert_ids[:, :, None] == jnp.arange(experts, dtype=jnp.int32)[None, None, :]
    named = jnp.sum(jnp.where(chosen, combine[:, :, None], 0.0), axis=1)
    high = named.astype(jnp.bfloat16)
    rest = (named - high.astype(jnp.float32)).astype(jnp.bfloat16)
    pad = jnp.zeros((tok, LANES * -(-2 * experts // LANES) - 2 * experts), jnp.bfloat16)
    first = jnp.concatenate([tokens, high, rest, pad], axis=1)

    def near_of(pieces):
        if nx == ny:
            lefts, rights = pieces[: nx - 1], pieces[nx - 1 :]
            return [jnp.concatenate([a, b], axis=1) for a, b in zip(lefts, rights)]
        return pieces

    def halves_of(near):
        if nx == ny:
            return [n[:, :half] for n in near], [n[:, half:] for n in near]
        return near[: nx - 1], near[nx - 1 :]

    near = [shift(tokens[:, :half], "e_lo", j) for j in range(1, nx)]
    near += [shift(first[:, half:], "e_hi", j) for j in range(1, ny)]
    near = near_of(near)

    own = [w.reshape(per_group * units, depth) for w in (gate_weight, up_weight, down_weight)]
    other = [shift(own[0], "core", 1)]

    def add(*terms):
        return sum(t.astype(jnp.float32) for t in terms)

    def exchange(first, near):
        lefts, rights = halves_of(near)
        left = jnp.concatenate([first[:, :half], *lefts])
        right = jnp.concatenate([first[:, half:], *rights])
        return (
            [shift(left, "e_hi", j) for j in range(1, ny)],
            [shift(right, "e_lo", j) for j in range(1, nx)],
        )

    def run(first, near, sides, *earlier):
        first, sides = after((first, sides), *earlier)
        if nx == ny:
            lefts, rights = halves_of(near)
            near = lefts + rights
        return ffn(first, near, *sides, weights, group, experts, per_group)

    def start_sums(parts, *earlier):
        send_a, keep_a, send_b, keep_b = parts
        send_a, send_b = after((send_a, send_b), *earlier)
        got_a = [shift(send_a[j - 1], "e_hi", -j) for j in range(1, ny)]
        got_b = [shift(send_b[j - 1], "e_lo", -j) for j in range(1, nx)]
        return [keep_a] + got_a, [keep_b] + got_b

    def finish_sums(terms_a, terms_b):
        sum_a = add(*terms_a).reshape(nx, tok, half)
        sum_b = add(*terms_b).reshape(ny, tok, half)
        last_a = [shift(sum_a[j].astype(jnp.bfloat16), "e_lo", -j) for j in range(1, nx)]
        last_b = [shift(sum_b[j].astype(jnp.bfloat16), "e_hi", -j) for j in range(1, ny)]
        return [sum_a[0]] + last_a, [sum_b[0]] + last_b

    firsts, nears, sides = [first], [near], [exchange(first, near)]
    firsts.append(ring_step(first))
    nears.append([ring_step(n) for n in near])
    other.append(shift(after(own[1], other[0], near, firsts[1]), "core", 1))
    other.append(shift(after(own[2], other[0], near, firsts[1]), "core", 1))
    weights = own + other

    parts, begun = {}, {}
    for k in range(1, stages):
        sides.append(exchange(firsts[k], nears[k]))
        if k + 1 < stages:
            if nx == ny:
                pair = jnp.concatenate([firsts[k], *nears[k]])
                pair = ring_step(pair)
                firsts.append(pair[:tok])
                nears.append([pair[i * tok : (i + 1) * tok] for i in range(1, nx)])
            else:
                firsts.append(ring_step(firsts[k]))
                nears.append([ring_step(n) for n in nears[k]])
        earlier = firsts[k], nears[k], begun.get(k - 2)
        parts[k - 1] = run(firsts[k - 1], nears[k - 1], sides[k - 1], *earlier)
        begun[k - 1] = start_sums(parts[k - 1], sides[k])
    last = stages - 1
    parts[last] = run(firsts[last], nears[last], sides[last], parts[last - 1])
    begun[last] = start_sums(parts[last], begun[last - 1])

    carry_a, carry_b = [], []
    for k in list(range(1, stages)) + [0]:
        terms_a, terms_b = begun[k]
        if k == 1:
            sums = jnp.concatenate([add(*terms_a), add(*terms_b)], axis=1 if nx == ny else 0)
            sums = ring_step(sums.astype(jnp.bfloat16))
            if nx == ny:
                mid_a, mid_b = [sums[:, :half]], [sums[:, half:]]
            else:
                mid_a, mid_b = [sums[: nx * tok]], [sums[nx * tok :]]
            continue
        if k == 0:
            mid_a, mid_b = [], []
        a, b = finish_sums(terms_a + mid_a, terms_b + mid_b)
        mid_a, mid_b = [], []
        total = jnp.concatenate([add(*a, *carry_a), add(*b, *carry_b)], axis=1)
        total = total.astype(jnp.bfloat16)
        if k:
            total = ring_step(total)
            carry_a, carry_b = [total[:, :half]], [total[:, half:]]
    return total


def solution(mesh):
    groups, shards = mesh.shape["expert"], mesh.shape["fsdp"]
    split = Mesh(mesh.devices.reshape(groups // 2, 2, shards // 2, 2), AXES)
    whole, expert, shard = P(AXES, None), ("e_hi", "e_lo"), ("line", "core")
    return jax.shard_map(
        per_device,
        mesh=split,
        in_specs=(whole, whole, whole) + (P(expert, shard, None),) * 3,
        out_specs=whole,
        check_vma=False,
    )
```

```python
import functools

import jax
import jax.numpy as jnp
from jax import lax
from jax.experimental import pallas as pl
from jax.experimental.pallas import tpu as pltpu
from jax.sharding import Mesh, PartitionSpec as P

AXES = ("e_hi", "e_lo", "line", "core")
LANES = 128
TILE = 256


def tiles(extent, size=TILE):
    return [(at, min(size, extent - at)) for at in range(0, extent, size)]


def ffn_kernel(ny, nx, experts, per_group, *refs):
    place, refs = refs[0], refs[1:]
    first, refs = refs[0], refs[1:]
    near, refs = refs[: nx + ny - 2], refs[nx + ny - 2 :]
    left, right, refs = refs[: ny - 1], refs[ny - 1 : ny + nx - 2], refs[ny + nx - 2 :]
    weights, refs = refs[:6], refs[6:]
    send_a, keep_a, send_b, keep_b = refs[:4]
    rows, hidden, row_sem = refs[4:]
    count, depth = rows.shape[0], weights[0].shape[0]
    half = depth // 2
    units = weights[2].shape[0]
    tok = count // (ny * nx)
    group = place[0]

    row_copies = []

    def bring(source, from_row, block, low):
        cols = pl.ds(0, half) if low else pl.ds(half, rows.shape[1] - half)
        from_cols = cols if source.shape[1] == rows.shape[1] else pl.ds(0, source.shape[1])
        row_copies.append(
            pltpu.make_async_copy(
                source.at[pl.ds(from_row, tok), from_cols],
                rows.at[pl.ds(block * tok, tok), cols],
                row_sem.at[len(row_copies)],
            )
        )

    for jy in range(ny):
        for jx in range(nx):
            block = jy * nx + jx
            if jy:
                bring(left[jy - 1], jx * tok, block, True)
            else:
                bring(near[jx - 1] if jx else first, 0, block, True)
            if jx:
                bring(right[jx - 1], jy * tok, block, False)
            else:
                bring(near[nx - 1 + jy - 1] if jy else first, 0, block, False)
    for copy in row_copies:
        copy.start()
    for copy in row_copies:
        copy.wait()

    extra = rows[:, depth:].astype(jnp.float32)
    lane = lax.broadcasted_iota(jnp.int32, extra.shape, 1)
    named = []
    for e in range(per_group):
        mine = group * per_group + e
        pick = (lane == mine) | (lane == mine + experts)
        named.append(0.5 * jnp.sum(jnp.where(pick, extra, 0.0), axis=1, keepdims=True))

    per_expert = units // per_group
    for h in range(2):
        gate, up = weights[3 * h], weights[3 * h + 1]
        for start, size in tiles(units):
            cols = slice(start, start + size)
            gate_pre = jnp.dot(rows[:, :depth], gate[:, cols], preferred_element_type=jnp.float32)
            up_pre = jnp.dot(rows[:, :depth], up[:, cols], preferred_element_type=jnp.float32)
            low, high = start // per_expert, (start + size - 1) // per_expert
            column = lax.broadcasted_iota(jnp.int32, (1, size), 1) + start
            scale = named[high]
            for e in range(high - 1, low - 1, -1):
                scale = jnp.where(column < (e + 1) * per_expert, named[e], scale)
            value = gate_pre * (1.0 + jnp.tanh(0.5 * gate_pre)) * (up_pre * scale)
            hidden[h, :, start : start + size] = value.astype(jnp.bfloat16)
    for start, size in tiles(depth):
        part = sum(
            jnp.dot(
                hidden[h],
                weights[3 * h + 2][:, start : start + size],
                preferred_element_type=jnp.float32,
            )
            for h in range(2)
        )
        to = slice(start % half, start % half + size)
        for jy in range(ny):
            for jx in range(nx):
                at = (jy * nx + jx) * tok
                block = part[at : at + tok]
                if start < half:
                    there = slice(jx * tok, (jx + 1) * tok)
                    if jy:
                        send_a[jy - 1, there, to] = block.astype(jnp.bfloat16)
                    else:
                        keep_a[there, to] = block
                else:
                    there = slice(jy * tok, (jy + 1) * tok)
                    if jx:
                        send_b[jx - 1, there, to] = block.astype(jnp.bfloat16)
                    else:
                        keep_b[there, to] = block


def turn_kernel(source, target):
    for start, size in tiles(source.shape[1]):
        target[start : start + size, :] = source[:, start : start + size].T


def turn(weight):
    vmem = pl.BlockSpec(memory_space=pltpu.VMEM)
    return pl.pallas_call(
        turn_kernel,
        in_specs=[vmem],
        out_specs=vmem,
        out_shape=jax.ShapeDtypeStruct(weight.shape[::-1], weight.dtype),
        compiler_params=pltpu.CompilerParams(vmem_limit_bytes=16 * 1024 * 1024),
        cost_estimate=pl.CostEstimate(
            flops=0, bytes_accessed=4 * weight.size, transcendentals=0
        ),
    )(weight)


def ffn(first, near, left, right, weights, place, experts, per_group):
    ny, nx = len(left) + 1, len(right) + 1
    tok, width = first.shape
    units, depth = weights[2].shape
    half, count = depth // 2, ny * nx * tok
    any_spec, vmem = pl.BlockSpec(memory_space=pl.ANY), pl.BlockSpec(memory_space=pltpu.VMEM)
    sources = [first, *near, *left, *right]
    macs = count * depth * units * 6
    return pl.pallas_call(
        functools.partial(ffn_kernel, ny, nx, experts, per_group),
        in_specs=[pl.BlockSpec(memory_space=pltpu.SMEM)] + [any_spec] * len(sources) + [vmem] * 6,
        out_specs=[vmem] * 4,
        out_shape=[
            jax.ShapeDtypeStruct((ny - 1, nx * tok, half), jnp.bfloat16),
            jax.ShapeDtypeStruct((nx * tok, half), jnp.float32),
            jax.ShapeDtypeStruct((nx - 1, ny * tok, half), jnp.bfloat16),
            jax.ShapeDtypeStruct((ny * tok, half), jnp.float32),
        ],
        scratch_shapes=[
            pltpu.VMEM((count, width), jnp.bfloat16),
            pltpu.VMEM((2, count, units), jnp.bfloat16),
            pltpu.SemaphoreType.DMA((2 * ny * nx,)),
        ],
        compiler_params=pltpu.CompilerParams(vmem_limit_bytes=26 * 1024 * 1024),
        cost_estimate=pl.CostEstimate(
            flops=2 * macs,
            bytes_accessed=8 * count * depth,
            transcendentals=2 * count * units,
        ),
    )(place, *sources, *weights)


def shift(value, axis, by):
    n = lax.axis_size(axis)
    return lax.ppermute(value, axis, [(i, (i + by) % n) for i in range(n)])


def ring_step(value):
    n = lax.axis_size("line")
    order = list(range(1, n, 2)) + list(range(0, n, 2))[::-1]
    return lax.ppermute(value, "line", [(order[i], order[(i + 1) % n]) for i in range(n)])


def after(value, *earlier):
    return lax.optimization_barrier((value, earlier))[0]


def per_device(tokens, expert_ids, combine, gate_weight, up_weight, down_weight):
    ny, nx, stages = lax.axis_size("e_hi"), lax.axis_size("e_lo"), lax.axis_size("line")
    per_group, units, depth = gate_weight.shape
    experts = ny * nx * per_group
    tok = tokens.shape[0]
    half = depth // 2
    group = lax.axis_index(("e_hi", "e_lo")).astype(jnp.int32).reshape(1)

    chosen = expert_ids[:, :, None] == jnp.arange(experts, dtype=jnp.int32)[None, None, :]
    named = jnp.sum(jnp.where(chosen, combine[:, :, None], 0.0), axis=1)
    high = named.astype(jnp.bfloat16)
    rest = (named - high.astype(jnp.float32)).astype(jnp.bfloat16)
    pad = jnp.zeros((tok, LANES * -(-2 * experts // LANES) - 2 * experts), jnp.bfloat16)
    first = jnp.concatenate([tokens, high, rest, pad], axis=1)

    def near_of(pieces):
        if nx == ny:
            lefts, rights = pieces[: nx - 1], pieces[nx - 1 :]
            return [jnp.concatenate([a, b], axis=1) for a, b in zip(lefts, rights)]
        return pieces

    def halves_of(near):
        if nx == ny:
            return [n[:, :half] for n in near], [n[:, half:] for n in near]
        return near[: nx - 1], near[nx - 1 :]

    near = [shift(tokens[:, :half], "e_lo", j) for j in range(1, nx)]
    near += [shift(first[:, half:], "e_hi", j) for j in range(1, ny)]
    near = near_of(near)

    own = [w.reshape(per_group * units, depth) for w in (gate_weight, up_weight, down_weight)]
    def add(*terms):
        return sum(t.astype(jnp.float32) for t in terms)

    def exchange(first, near):
        lefts, rights = halves_of(near)
        left = jnp.concatenate([first[:, :half], *lefts])
        right = jnp.concatenate([first[:, half:], *rights])
        return (
            [shift(left, "e_hi", j) for j in range(1, ny)],
            [shift(right, "e_lo", j) for j in range(1, nx)],
        )

    def run(first, near, sides, *earlier):
        first, sides = after((first, sides), *earlier)
        if nx == ny:
            lefts, rights = halves_of(near)
            near = lefts + rights
        return ffn(first, near, *sides, weights, group, experts, per_group)

    def start_sums(parts, *earlier):
        send_a, keep_a, send_b, keep_b = parts
        send_a, send_b = after((send_a, send_b), *earlier)
        got_a = [shift(send_a[j - 1], "e_hi", -j) for j in range(1, ny)]
        got_b = [shift(send_b[j - 1], "e_lo", -j) for j in range(1, nx)]
        return [keep_a] + got_a, [keep_b] + got_b

    def finish_sums(terms_a, terms_b):
        sum_a = add(*terms_a).reshape(nx, tok, half)
        sum_b = add(*terms_b).reshape(ny, tok, half)
        last_a = [shift(sum_a[j].astype(jnp.bfloat16), "e_lo", -j) for j in range(1, nx)]
        last_b = [shift(sum_b[j].astype(jnp.bfloat16), "e_hi", -j) for j in range(1, ny)]
        return [sum_a[0]] + last_a, [sum_b[0]] + last_b

    firsts, nears, sides = [first], [near], [exchange(first, near)]
    firsts.append(ring_step(first))
    nears.append([ring_step(n) for n in near])
    own = [turn(own[0]), turn(own[1]), own[2]]
    other_down = shift(own[2], "core", 1)
    turned = after(own[:2], other_down, near, firsts[1])
    weights = own + [shift(w, "core", 1) for w in turned] + [other_down]

    parts, begun = {}, {}
    for k in range(1, stages):
        sides.append(exchange(firsts[k], nears[k]))
        if k + 1 < stages:
            if nx == ny:
                pair = jnp.concatenate([firsts[k], *nears[k]])
                pair = ring_step(pair)
                firsts.append(pair[:tok])
                nears.append([pair[i * tok : (i + 1) * tok] for i in range(1, nx)])
            else:
                firsts.append(ring_step(firsts[k]))
                nears.append([ring_step(n) for n in nears[k]])
        earlier = firsts[k], nears[k], begun.get(k - 2)
        parts[k - 1] = run(firsts[k - 1], nears[k - 1], sides[k - 1], *earlier)
        begun[k - 1] = start_sums(parts[k - 1], sides[k])
    last = stages - 1
    parts[last] = run(firsts[last], nears[last], sides[last], parts[last - 1])
    begun[last] = start_sums(parts[last], begun[last - 1])

    carry_a, carry_b = [], []
    for k in list(range(1, stages)) + [0]:
        terms_a, terms_b = begun[k]
        if k == 1:
            sums = jnp.concatenate([add(*terms_a), add(*terms_b)], axis=1 if nx == ny else 0)
            sums = ring_step(sums.astype(jnp.bfloat16))
            if nx == ny:
                mid_a, mid_b = [sums[:, :half]], [sums[:, half:]]
            else:
                mid_a, mid_b = [sums[: nx * tok]], [sums[nx * tok :]]
            continue
        if k == 0:
            mid_a, mid_b = [], []
        a, b = finish_sums(terms_a + mid_a, terms_b + mid_b)
        mid_a, mid_b = [], []
        total = jnp.concatenate([add(*a, *carry_a), add(*b, *carry_b)], axis=1)
        total = total.astype(jnp.bfloat16)
        if k:
            total = ring_step(total)
            carry_a, carry_b = [total[:, :half]], [total[:, half:]]
    return total


def solution(mesh):
    groups, shards = mesh.shape["expert"], mesh.shape["fsdp"]
    split = Mesh(mesh.devices.reshape(groups // 2, 2, shards // 2, 2), AXES)
    whole, expert, shard = P(AXES, None), ("e_hi", "e_lo"), ("line", "core")
    return jax.shard_map(
        per_device,
        mesh=split,
        in_specs=(whole, whole, whole) + (P(expert, shard, None),) * 3,
        out_specs=whole,
        check_vma=False,
    )
```

```python
import functools

import jax
import jax.numpy as jnp
from jax import lax
from jax.experimental import pallas as pl
from jax.experimental.pallas import tpu as pltpu
from jax.sharding import Mesh, PartitionSpec as P

AXES = ("e_hi", "e_lo", "line", "core")
LANES = 128
TILE = 256


def tiles(extent, size=TILE):
    return [(at, min(size, extent - at)) for at in range(0, extent, size)]


def ffn_kernel(ny, nx, experts, per_group, *refs):
    place, refs = refs[0], refs[1:]
    first, refs = refs[0], refs[1:]
    near, refs = refs[: nx + ny - 2], refs[nx + ny - 2 :]
    left, right, refs = refs[: ny - 1], refs[ny - 1 : ny + nx - 2], refs[ny + nx - 2 :]
    weights, refs = refs[:6], refs[6:]
    send_a, keep_a, send_b, keep_b = refs[:4]
    rows, hidden, row_sem = refs[4:]
    count, depth = rows.shape[0], weights[0].shape[1]
    half = depth // 2
    units = weights[0].shape[0]
    tok = count // (ny * nx)
    group = place[0]

    row_copies = []

    def bring(source, from_row, block, low):
        cols = pl.ds(0, half) if low else pl.ds(half, rows.shape[1] - half)
        from_cols = cols if source.shape[1] == rows.shape[1] else pl.ds(0, source.shape[1])
        row_copies.append(
            pltpu.make_async_copy(
                source.at[pl.ds(from_row, tok), from_cols],
                rows.at[pl.ds(block * tok, tok), cols],
                row_sem.at[len(row_copies)],
            )
        )

    for jy in range(ny):
        for jx in range(nx):
            block = jy * nx + jx
            if jy:
                bring(left[jy - 1], jx * tok, block, True)
            else:
                bring(near[jx - 1] if jx else first, 0, block, True)
            if jx:
                bring(right[jx - 1], jy * tok, block, False)
            else:
                bring(near[nx - 1 + jy - 1] if jy else first, 0, block, False)
    for copy in row_copies:
        copy.start()
    for copy in row_copies:
        copy.wait()

    extra = rows[:, depth:].astype(jnp.float32)
    lane = lax.broadcasted_iota(jnp.int32, extra.shape, 1)
    named = []
    for e in range(per_group):
        mine = group * per_group + e
        pick = (lane == mine) | (lane == mine + experts)
        named.append(0.5 * jnp.sum(jnp.where(pick, extra, 0.0), axis=1, keepdims=True))

    per_expert = units // per_group
    nt = (((1,), (1,)), ((), ()))
    for h in range(2):
        gate, up = weights[3 * h], weights[3 * h + 1]
        for start, size in tiles(units):
            gate_pre = lax.dot_general(
                rows[:, :depth],
                gate[start : start + size],
                nt,
                preferred_element_type=jnp.float32,
            )
            up_pre = lax.dot_general(
                rows[:, :depth],
                up[start : start + size],
                nt,
                preferred_element_type=jnp.float32,
            )
            low, high = start // per_expert, (start + size - 1) // per_expert
            column = lax.broadcasted_iota(jnp.int32, (1, size), 1) + start
            scale = named[high]
            for e in range(high - 1, low - 1, -1):
                scale = jnp.where(column < (e + 1) * per_expert, named[e], scale)
            value = gate_pre * (1.0 + jnp.tanh(0.5 * gate_pre)) * (up_pre * scale)
            hidden[h, :, start : start + size] = value.astype(jnp.bfloat16)
    for start, size in tiles(depth):
        part = sum(
            jnp.dot(
                hidden[h],
                weights[3 * h + 2][:, start : start + size],
                preferred_element_type=jnp.float32,
            )
            for h in range(2)
        )
        to = slice(start % half, start % half + size)
        for jy in range(ny):
            for jx in range(nx):
                at = (jy * nx + jx) * tok
                block = part[at : at + tok]
                if start < half:
                    there = slice(jx * tok, (jx + 1) * tok)
                    if jy:
                        send_a[jy - 1, there, to] = block.astype(jnp.bfloat16)
                    else:
                        keep_a[there, to] = block
                else:
                    there = slice(jy * tok, (jy + 1) * tok)
                    if jx:
                        send_b[jx - 1, there, to] = block.astype(jnp.bfloat16)
                    else:
                        keep_b[there, to] = block


def ffn(first, near, left, right, weights, place, experts, per_group):
    ny, nx = len(left) + 1, len(right) + 1
    tok, width = first.shape
    units, depth = weights[0].shape
    half, count = depth // 2, ny * nx * tok
    any_spec, vmem = pl.BlockSpec(memory_space=pl.ANY), pl.BlockSpec(memory_space=pltpu.VMEM)
    sources = [first, *near, *left, *right]
    macs = count * depth * units * 6
    return pl.pallas_call(
        functools.partial(ffn_kernel, ny, nx, experts, per_group),
        in_specs=[pl.BlockSpec(memory_space=pltpu.SMEM)] + [any_spec] * len(sources) + [vmem] * 6,
        out_specs=[vmem] * 4,
        out_shape=[
            jax.ShapeDtypeStruct((ny - 1, nx * tok, half), jnp.bfloat16),
            jax.ShapeDtypeStruct((nx * tok, half), jnp.float32),
            jax.ShapeDtypeStruct((nx - 1, ny * tok, half), jnp.bfloat16),
            jax.ShapeDtypeStruct((ny * tok, half), jnp.float32),
        ],
        scratch_shapes=[
            pltpu.VMEM((count, width), jnp.bfloat16),
            pltpu.VMEM((2, count, units), jnp.bfloat16),
            pltpu.SemaphoreType.DMA((2 * ny * nx,)),
        ],
        compiler_params=pltpu.CompilerParams(vmem_limit_bytes=26 * 1024 * 1024),
        cost_estimate=pl.CostEstimate(
            flops=macs // 1000,
            bytes_accessed=count,
            transcendentals=0,
        ),
    )(place, *sources, *weights)


def shift(value, axis, by):
    n = lax.axis_size(axis)
    return lax.ppermute(value, axis, [(i, (i + by) % n) for i in range(n)])


def ring_step(value):
    n = lax.axis_size("line")
    order = list(range(1, n, 2)) + list(range(0, n, 2))[::-1]
    return lax.ppermute(value, "line", [(order[i], order[(i + 1) % n]) for i in range(n)])


def after(value, *earlier):
    return lax.optimization_barrier((value, earlier))[0]


def per_device(tokens, expert_ids, combine, gate_weight, up_weight, down_weight):
    ny, nx, stages = lax.axis_size("e_hi"), lax.axis_size("e_lo"), lax.axis_size("line")
    per_group, units, depth = gate_weight.shape
    experts = ny * nx * per_group
    tok = tokens.shape[0]
    half = depth // 2
    split = (tok // 2 + 15) // 16 * 16
    group = lax.axis_index(("e_hi", "e_lo")).astype(jnp.int32).reshape(1)

    chosen = expert_ids[:, :, None] == jnp.arange(experts, dtype=jnp.int32)[None, None, :]
    named = jnp.sum(jnp.where(chosen, combine[:, :, None], 0.0), axis=1)
    high = named.astype(jnp.bfloat16)
    rest = (named - high.astype(jnp.float32)).astype(jnp.bfloat16)
    pad = jnp.zeros((tok, LANES * -(-2 * experts // LANES) - 2 * experts), jnp.bfloat16)
    first = jnp.concatenate([tokens, high, rest, pad], axis=1)

    def add(*terms):
        return sum(t.astype(jnp.float32) for t in terms)

    seen = []

    def held(value):
        return after(value, list(seen)) if seen else value

    def wait(*values):
        seen.extend(values)

    def neighbours(axis, pieces, sign=1):
        return [shift(held(p), axis, sign * j) for j, p in enumerate(pieces, 1)]

    def near_of(lefts, rights):
        if nx == ny:
            return [jnp.concatenate([a, b], axis=1) for a, b in zip(lefts, rights)]
        return lefts + rights

    def halves_of(near):
        if nx == ny:
            return [n[:, :half] for n in near], [n[:, half:] for n in near]
        return near[: nx - 1], near[nx - 1 :]

    def opened(slot):
        slot = held(slot)
        if len(slot) > 1:
            return slot[0], slot[1:]
        n = slot[0].shape[0] // nx
        return slot[0][:n], [slot[0][i * n : (i + 1) * n] for i in range(1, nx)]

    def along(slot, low, high):
        first, near = opened(slot)
        arrays = [a[low:high] for a in [first, *near]]
        if nx == ny:
            arrays = [jnp.concatenate(arrays)]
        return [ring_step(a) for a in arrays]

    def to_y(slot):
        first, near = opened(slot)
        left = jnp.concatenate([first[:, :half], *halves_of(near)[0]])
        return [shift(left, "e_hi", j) for j in range(1, ny)]

    def to_x(slot):
        first, near = opened(slot)
        right = jnp.concatenate([first[:, half:], *halves_of(near)[1]])
        return [shift(right, "e_lo", j) for j in range(1, nx)]

    def exchange(slot):
        return to_y(slot), to_x(slot)

    def run(slot, sides):
        first, near = opened(slot)
        if nx == ny:
            lefts, rights = halves_of(near)
            near = lefts + rights
        parts = ffn(first, near, *held(sides), weights, group, experts, per_group)
        seen[:] = [parts]
        return parts

    def start_sums(parts):
        send_a, keep_a, send_b, keep_b = parts
        got_a = neighbours("e_hi", [send_a[j] for j in range(ny - 1)], -1)
        got_b = neighbours("e_lo", [send_b[j] for j in range(nx - 1)], -1)
        return [keep_a] + got_a, [keep_b] + got_b

    def finish_sums(terms):
        terms_a, terms_b = held(terms)
        sum_a = add(*terms_a).reshape(nx, -1, half)
        sum_b = add(*terms_b).reshape(ny, -1, half)
        last_a = [shift(sum_a[j].astype(jnp.bfloat16), "e_lo", -j) for j in range(1, nx)]
        last_b = [shift(sum_b[j].astype(jnp.bfloat16), "e_hi", -j) for j in range(1, ny)]
        return [sum_a[0]] + last_a, [sum_b[0]] + last_b

    def pass_on(terms):
        terms_a, terms_b = held(terms)
        sums = add(*terms_a), add(*terms_b)
        sums = ring_step(jnp.concatenate(sums, axis=1 if nx == ny else 0).astype(jnp.bfloat16))
        if nx == ny:
            return [sums[:, :half]], [sums[:, half:]]
        return [sums[: nx * tok]], [sums[nx * tok :]]

    def with_terms(terms, more):
        return terms[0] + more[0], terms[1] + more[1]

    def joined(low, high):
        def rows(part, count):
            return [t.reshape(count, -1, half) for t in part]

        sides = []
        for part_low, part_high, count in ((low[0], high[0], nx), (low[1], high[1], ny)):
            both = zip(rows(part_low, count), rows(part_high, count))
            sides.append([jnp.concatenate(b, axis=1).reshape(-1, half) for b in both])
        return sides

    def total_of(ended, *carry):
        ended, carry = held((ended, carry))
        a = add(*ended[0], *[c[:, :half] for c in carry])
        b = add(*ended[1], *[c[:, half:] for c in carry])
        return jnp.concatenate([a, b], axis=1).astype(jnp.bfloat16)

    own = [w.reshape(per_group * units, depth) for w in (gate_weight, up_weight, down_weight)]
    lefts = neighbours("e_lo", [tokens[:, :half]] * (nx - 1))
    next_first = ring_step(first)
    rights = neighbours("e_hi", [first[:, half:]] * (ny - 1))
    other = [shift(w, "core", 1) for w in own[:2]]
    near = near_of(lefts, rights)
    slot = [[first, *near]]
    wait(near)
    sides = [exchange(slot[0])]
    wait(next_first, other)
    next_near = [ring_step(held(n)) for n in near]
    other.append(shift(held(own[2]), "core", 1))
    wait(sides[0], next_near)
    weights = own + other
    slot.append([next_first, *next_near])
    begun, ended = {}, {}
    last = stages - 1

    for k in range(1, last):
        if k + 1 < last:
            slot.append(along(slot[k], 0, tok))
        else:
            low = along(slot[k], 0, split)
        sides.append(exchange(slot[k]))
        if k == 1:
            wait(other)
        parts = run(slot[k - 1], sides[k - 1])
        if k > 1:
            wait(begun[k - 2])
        if k + 1 == last:
            high = along(slot[k], split, tok)
            wait(low)
            low_sides = exchange(low)
        wait(sides[k])
        begun[k - 1] = start_sums(parts)
        if k + 1 < last:
            wait(slot[k + 1])
    parts = run(slot[last - 1], sides[last - 1])
    wait(high, low_sides)
    high_sides = exchange(high)
    wait(begun[last - 2])
    on_way = pass_on(begun[1])
    begun[last - 1] = start_sums(parts)
    parts = run(low, low_sides)
    wait(high_sides)
    low_sums = start_sums(parts)
    parts = run(high, high_sides)
    wait(begun[last - 1], on_way)
    ended = finish_sums(with_terms(begun[2], on_way))
    for k in range(3, last):
        wait(ended)
        moved = ring_step(total_of(ended))
        wait(moved)
        ended = finish_sums(begun[k])
        ended[0].append(moved[:, :half])
        ended[1].append(moved[:, half:])
    wait(low_sums)
    high_sums = start_sums(parts)
    wait(ended)
    carry = ring_step(total_of(ended))
    wait(high_sums)
    ends = finish_sums(joined(low_sums, high_sums))
    wait(carry, ends)
    carry = ring_step(total_of(ends, carry))
    ended = finish_sums(begun[0])
    return total_of(ended, carry)


def solution(mesh):
    groups, shards = mesh.shape["expert"], mesh.shape["fsdp"]
    split = Mesh(mesh.devices.reshape(groups // 2, 2, shards // 2, 2), AXES)
    whole, expert, shard = P(AXES, None), ("e_hi", "e_lo"), ("line", "core")
    return jax.shard_map(
        per_device,
        mesh=split,
        in_specs=(whole, whole, whole) + (P(expert, shard, None),) * 3,
        out_specs=whole,
        check_vma=False,
    )
```

```python
import functools

import jax
import jax.numpy as jnp
from jax import lax
from jax.experimental import pallas as pl
from jax.experimental.pallas import tpu as pltpu
from jax.sharding import Mesh, PartitionSpec as P

AXES = ("e_hi", "e_lo", "line", "core")
LANES = 128
TILE = 256


def tiles(extent, size=TILE):
    return [(at, min(size, extent - at)) for at in range(0, extent, size)]


def ffn_kernel(ny, nx, experts, per_group, *refs):
    place, refs = refs[0], refs[1:]
    first, refs = refs[0], refs[1:]
    near, refs = refs[: nx + ny - 2], refs[nx + ny - 2 :]
    left, right, refs = refs[: ny - 1], refs[ny - 1 : ny + nx - 2], refs[ny + nx - 2 :]
    weights, refs = refs[:6], refs[6:]
    send_a, keep_a, send_b, keep_b = refs[:4]
    rows, hidden, row_sem = refs[4:]
    count, depth = rows.shape[0], weights[0].shape[1]
    half = depth // 2
    units = weights[0].shape[0]
    tok = count // (ny * nx)
    group = place[0]

    row_copies = []

    def bring(source, from_row, block, low):
        cols = pl.ds(0, half) if low else pl.ds(half, rows.shape[1] - half)
        from_cols = cols if source.shape[1] == rows.shape[1] else pl.ds(0, source.shape[1])
        row_copies.append(
            pltpu.make_async_copy(
                source.at[pl.ds(from_row, tok), from_cols],
                rows.at[pl.ds(block * tok, tok), cols],
                row_sem.at[len(row_copies)],
            )
        )

    for jy in range(ny):
        for jx in range(nx):
            block = jy * nx + jx
            if jy:
                bring(left[jy - 1], jx * tok, block, True)
            else:
                bring(near[jx - 1] if jx else first, 0, block, True)
            if jx:
                bring(right[jx - 1], jy * tok, block, False)
            else:
                bring(near[nx - 1 + jy - 1] if jy else first, 0, block, False)
    for copy in row_copies:
        copy.start()
    for copy in row_copies:
        copy.wait()

    extra = rows[:, depth:].astype(jnp.float32)
    lane = lax.broadcasted_iota(jnp.int32, extra.shape, 1)
    named = []
    for e in range(per_group):
        mine = group * per_group + e
        pick = (lane == mine) | (lane == mine + experts)
        named.append(0.5 * jnp.sum(jnp.where(pick, extra, 0.0), axis=1, keepdims=True))

    per_expert = units // per_group
    nt = (((1,), (1,)), ((), ()))
    for h in range(2):
        gate, up = weights[3 * h], weights[3 * h + 1]
        for start, size in tiles(units):
            gate_pre = lax.dot_general(
                rows[:, :depth],
                gate[start : start + size],
                nt,
                preferred_element_type=jnp.float32,
            )
            up_pre = lax.dot_general(
                rows[:, :depth],
                up[start : start + size],
                nt,
                preferred_element_type=jnp.float32,
            )
            low, high = start // per_expert, (start + size - 1) // per_expert
            column = lax.broadcasted_iota(jnp.int32, (1, size), 1) + start
            scale = named[high]
            for e in range(high - 1, low - 1, -1):
                scale = jnp.where(column < (e + 1) * per_expert, named[e], scale)
            value = gate_pre * (1.0 + jnp.tanh(0.5 * gate_pre)) * (up_pre * scale)
            hidden[h, :, start : start + size] = value.astype(jnp.bfloat16)
    for start, size in tiles(depth):
        part = sum(
            jnp.dot(
                hidden[h],
                weights[3 * h + 2][:, start : start + size],
                preferred_element_type=jnp.float32,
            )
            for h in range(2)
        )
        to = slice(start % half, start % half + size)
        for jy in range(ny):
            for jx in range(nx):
                at = (jy * nx + jx) * tok
                block = part[at : at + tok]
                if start < half:
                    there = slice(jx * tok, (jx + 1) * tok)
                    if jy:
                        send_a[jy - 1, there, to] = block.astype(jnp.bfloat16)
                    else:
                        keep_a[there, to] = block
                else:
                    there = slice(jy * tok, (jy + 1) * tok)
                    if jx:
                        send_b[jx - 1, there, to] = block.astype(jnp.bfloat16)
                    else:
                        keep_b[there, to] = block


def ffn(first, near, left, right, weights, place, experts, per_group):
    ny, nx = len(left) + 1, len(right) + 1
    tok, width = first.shape
    units, depth = weights[0].shape
    half, count = depth // 2, ny * nx * tok
    any_spec, vmem = pl.BlockSpec(memory_space=pl.ANY), pl.BlockSpec(memory_space=pltpu.VMEM)
    sources = [first, *near, *left, *right]
    macs = count * depth * units * 6
    return pl.pallas_call(
        functools.partial(ffn_kernel, ny, nx, experts, per_group),
        in_specs=[pl.BlockSpec(memory_space=pltpu.SMEM)] + [any_spec] * len(sources) + [vmem] * 6,
        out_specs=[vmem] * 4,
        out_shape=[
            jax.ShapeDtypeStruct((ny - 1, nx * tok, half), jnp.bfloat16),
            jax.ShapeDtypeStruct((nx * tok, half), jnp.float32),
            jax.ShapeDtypeStruct((nx - 1, ny * tok, half), jnp.bfloat16),
            jax.ShapeDtypeStruct((ny * tok, half), jnp.float32),
        ],
        scratch_shapes=[
            pltpu.VMEM((count, width), jnp.bfloat16),
            pltpu.VMEM((2, count, units), jnp.bfloat16),
            pltpu.SemaphoreType.DMA((2 * ny * nx,)),
        ],
        compiler_params=pltpu.CompilerParams(vmem_limit_bytes=14 * 1024 * 1024),
        cost_estimate=pl.CostEstimate(
            flops=macs // 1000,
            bytes_accessed=count,
            transcendentals=0,
        ),
    )(place, *sources, *weights)


def shift(value, axis, by):
    n = lax.axis_size(axis)
    return lax.ppermute(value, axis, [(i, (i + by) % n) for i in range(n)])


def ring_step(value):
    n = lax.axis_size("line")
    order = list(range(1, n, 2)) + list(range(0, n, 2))[::-1]
    return lax.ppermute(value, "line", [(order[i], order[(i + 1) % n]) for i in range(n)])


def after(value, *earlier):
    return lax.optimization_barrier((value, earlier))[0]


def per_device(tokens, expert_ids, combine, gate_weight, up_weight, down_weight):
    ny, nx, stages = lax.axis_size("e_hi"), lax.axis_size("e_lo"), lax.axis_size("line")
    per_group, units, depth = gate_weight.shape
    experts = ny * nx * per_group
    tok = tokens.shape[0]
    half = depth // 2
    split = (tok // 2 + 15) // 16 * 16
    group = lax.axis_index(("e_hi", "e_lo")).astype(jnp.int32).reshape(1)

    chosen = expert_ids[:, :, None] == jnp.arange(experts, dtype=jnp.int32)[None, None, :]
    named = jnp.sum(jnp.where(chosen, combine[:, :, None], 0.0), axis=1)
    high = named.astype(jnp.bfloat16)
    rest = (named - high.astype(jnp.float32)).astype(jnp.bfloat16)
    pad = jnp.zeros((tok, LANES * -(-2 * experts // LANES) - 2 * experts), jnp.bfloat16)
    first = jnp.concatenate([tokens, high, rest, pad], axis=1)

    def add(*terms):
        return sum(t.astype(jnp.float32) for t in terms)

    seen = []

    def held(value):
        return after(value, list(seen)) if seen else value

    def wait(*values):
        seen.extend(values)

    def neighbours(axis, pieces, sign=1):
        return [shift(held(p), axis, sign * j) for j, p in enumerate(pieces, 1)]

    def near_of(lefts, rights):
        if nx == ny:
            return [jnp.concatenate([a, b], axis=1) for a, b in zip(lefts, rights)]
        return lefts + rights

    def halves_of(near):
        if nx == ny:
            return [n[:, :half] for n in near], [n[:, half:] for n in near]
        return near[: nx - 1], near[nx - 1 :]

    def opened(slot):
        slot = held(slot)
        if len(slot) > 1:
            return slot[0], slot[1:]
        n = slot[0].shape[0] // nx
        return slot[0][:n], [slot[0][i * n : (i + 1) * n] for i in range(1, nx)]

    def along(slot, low, high):
        first, near = opened(slot)
        arrays = [a[low:high] for a in [first, *near]]
        if nx == ny:
            arrays = [jnp.concatenate(arrays)]
        return [ring_step(a) for a in arrays]

    def to_y(slot):
        first, near = opened(slot)
        left = jnp.concatenate([first[:, :half], *halves_of(near)[0]])
        return [shift(left, "e_hi", j) for j in range(1, ny)]

    def to_x(slot):
        first, near = opened(slot)
        right = jnp.concatenate([first[:, half:], *halves_of(near)[1]])
        return [shift(right, "e_lo", j) for j in range(1, nx)]

    def exchange(slot):
        return to_y(slot), to_x(slot)

    def run(slot, sides):
        first, near = opened(slot)
        if nx == ny:
            lefts, rights = halves_of(near)
            near = lefts + rights
        parts = ffn(first, near, *held(sides), weights, group, experts, per_group)
        seen[:] = [parts]
        return parts

    def start_sums(parts):
        send_a, keep_a, send_b, keep_b = parts
        got_a = neighbours("e_hi", [send_a[j] for j in range(ny - 1)], -1)
        got_b = neighbours("e_lo", [send_b[j] for j in range(nx - 1)], -1)
        return [keep_a] + got_a, [keep_b] + got_b

    def finish_sums(terms):
        terms_a, terms_b = held(terms)
        sum_a = add(*terms_a).reshape(nx, -1, half)
        sum_b = add(*terms_b).reshape(ny, -1, half)
        last_a = [shift(sum_a[j].astype(jnp.bfloat16), "e_lo", -j) for j in range(1, nx)]
        last_b = [shift(sum_b[j].astype(jnp.bfloat16), "e_hi", -j) for j in range(1, ny)]
        return [sum_a[0]] + last_a, [sum_b[0]] + last_b

    def pass_on(terms):
        terms_a, terms_b = held(terms)
        sums = add(*terms_a), add(*terms_b)
        sums = ring_step(jnp.concatenate(sums, axis=1 if nx == ny else 0).astype(jnp.bfloat16))
        if nx == ny:
            return [sums[:, :half]], [sums[:, half:]]
        return [sums[: nx * tok]], [sums[nx * tok :]]

    def with_terms(terms, more):
        return terms[0] + more[0], terms[1] + more[1]

    def joined(low, high):
        def rows(part, count):
            return [t.reshape(count, -1, half) for t in part]

        sides = []
        for part_low, part_high, count in ((low[0], high[0], nx), (low[1], high[1], ny)):
            both = zip(rows(part_low, count), rows(part_high, count))
            sides.append([jnp.concatenate(b, axis=1).reshape(-1, half) for b in both])
        return sides

    def total_of(ended, *carry):
        ended, carry = held((ended, carry))
        a = add(*ended[0], *[c[:, :half] for c in carry])
        b = add(*ended[1], *[c[:, half:] for c in carry])
        return jnp.concatenate([a, b], axis=1).astype(jnp.bfloat16)

    own = [w.reshape(per_group * units, depth) for w in (gate_weight, up_weight, down_weight)]
    lefts = neighbours("e_lo", [tokens[:, :half]] * (nx - 1))
    next_first = ring_step(first)
    rights = neighbours("e_hi", [first[:, half:]] * (ny - 1))
    other = [shift(w, "core", 1) for w in own[:2]]
    near = near_of(lefts, rights)
    slot = [[first, *near]]
    wait(near)
    sides = [exchange(slot[0])]
    wait(next_first, other)
    next_near = [ring_step(held(n)) for n in near]
    other.append(shift(held(own[2]), "core", 1))
    wait(sides[0], next_near)
    weights = own + other
    slot.append([next_first, *next_near])
    begun, ended = {}, {}
    last = stages - 1

    for k in range(1, last):
        if k + 1 < last:
            slot.append(along(slot[k], 0, tok))
        else:
            low = along(slot[k], 0, split)
        sides.append(exchange(slot[k]))
        if k == 1:
            wait(other)
        parts = run(slot[k - 1], sides[k - 1])
        if k > 1:
            wait(begun[k - 2])
        if k + 1 == last:
            high = along(slot[k], split, tok)
            wait(low)
            low_sides = exchange(low)
        wait(sides[k])
        begun[k - 1] = start_sums(parts)
        if k + 1 < last:
            wait(slot[k + 1])
    parts = run(slot[last - 1], sides[last - 1])
    wait(high, low_sides)
    high_sides = exchange(high)
    wait(begun[last - 2])
    on_way = pass_on(begun[1])
    begun[last - 1] = start_sums(parts)
    parts = run(low, low_sides)
    wait(high_sides)
    low_sums = start_sums(parts)
    parts = run(high, high_sides)
    wait(begun[last - 1], on_way)
    ended = finish_sums(with_terms(begun[2], on_way))
    for k in range(3, last):
        wait(ended)
        moved = ring_step(total_of(ended))
        wait(moved)
        ended = finish_sums(begun[k])
        ended[0].append(moved[:, :half])
        ended[1].append(moved[:, half:])
    wait(low_sums)
    high_sums = start_sums(parts)
    wait(ended)
    carry = ring_step(total_of(ended))
    wait(high_sums)
    ends = finish_sums(joined(low_sums, high_sums))
    wait(carry, ends)
    carry = ring_step(total_of(ends, carry))
    ended = finish_sums(begun[0])
    return total_of(ended, carry)


def solution(mesh):
    groups, shards = mesh.shape["expert"], mesh.shape["fsdp"]
    split = Mesh(mesh.devices.reshape(groups // 2, 2, shards // 2, 2), AXES)
    whole, expert, shard = P(AXES, None), ("e_hi", "e_lo"), ("line", "core")
    return jax.shard_map(
        per_device,
        mesh=split,
        in_specs=(whole, whole, whole) + (P(expert, shard, None),) * 3,
        out_specs=whole,
        check_vma=False,
    )
```

```python
import functools

import jax
import jax.numpy as jnp
from jax import lax
from jax.experimental import pallas as pl
from jax.experimental.pallas import tpu as pltpu
from jax.sharding import Mesh, PartitionSpec as P

AXES = ("e_hi", "e_lo", "line", "core")
LANES = 128
TILE = 256


def tiles(extent, size=TILE):
    return [(at, min(size, extent - at)) for at in range(0, extent, size)]


def ffn_kernel(ny, nx, experts, per_group, *refs):
    place, refs = refs[0], refs[1:]
    first, refs = refs[0], refs[1:]
    near, refs = refs[: nx + ny - 2], refs[nx + ny - 2 :]
    left, right, refs = refs[: ny - 1], refs[ny - 1 : ny + nx - 2], refs[ny + nx - 2 :]
    weights, refs = refs[:6], refs[6:]
    send_a, keep_a, send_b, keep_b = refs[:4]
    rows, hidden, row_sem = refs[4:]
    count, depth = rows.shape[0], weights[0].shape[1]
    half = depth // 2
    units = weights[0].shape[0]
    tok = count // (ny * nx)
    group = place[0]

    row_copies = []

    def bring(source, from_row, block, low):
        cols = pl.ds(0, half) if low else pl.ds(half, rows.shape[1] - half)
        from_cols = cols if source.shape[1] == rows.shape[1] else pl.ds(0, source.shape[1])
        row_copies.append(
            pltpu.make_async_copy(
                source.at[pl.ds(from_row, tok), from_cols],
                rows.at[pl.ds(block * tok, tok), cols],
                row_sem.at[len(row_copies)],
            )
        )

    for jy in range(ny):
        for jx in range(nx):
            block = jy * nx + jx
            if jy:
                bring(left[jy - 1], jx * tok, block, True)
            else:
                bring(near[jx - 1] if jx else first, 0, block, True)
            if jx:
                bring(right[jx - 1], jy * tok, block, False)
            else:
                bring(near[nx - 1 + jy - 1] if jy else first, 0, block, False)
    for copy in row_copies:
        copy.start()
    for copy in row_copies:
        copy.wait()

    extra = rows[:, depth:].astype(jnp.float32)
    lane = lax.broadcasted_iota(jnp.int32, extra.shape, 1)
    named = []
    for e in range(per_group):
        mine = group * per_group + e
        pick = (lane == mine) | (lane == mine + experts)
        named.append(0.5 * jnp.sum(jnp.where(pick, extra, 0.0), axis=1, keepdims=True))

    per_expert = units // per_group
    nt = (((1,), (1,)), ((), ()))
    for h in range(2):
        gate, up = weights[3 * h], weights[3 * h + 1]
        for start, size in tiles(units):
            gate_pre = lax.dot_general(
                rows[:, :depth],
                gate[start : start + size],
                nt,
                preferred_element_type=jnp.float32,
            )
            up_pre = lax.dot_general(
                rows[:, :depth],
                up[start : start + size],
                nt,
                preferred_element_type=jnp.float32,
            )
            low, high = start // per_expert, (start + size - 1) // per_expert
            column = lax.broadcasted_iota(jnp.int32, (1, size), 1) + start
            scale = named[high]
            for e in range(high - 1, low - 1, -1):
                scale = jnp.where(column < (e + 1) * per_expert, named[e], scale)
            value = gate_pre * (1.0 + jnp.tanh(0.5 * gate_pre)) * (up_pre * scale)
            hidden[h, :, start : start + size] = value.astype(jnp.bfloat16)
    for start, size in tiles(depth):
        part = sum(
            jnp.dot(
                hidden[h],
                weights[3 * h + 2][:, start : start + size],
                preferred_element_type=jnp.float32,
            )
            for h in range(2)
        )
        to = slice(start % half, start % half + size)
        for jy in range(ny):
            for jx in range(nx):
                at = (jy * nx + jx) * tok
                block = part[at : at + tok]
                if start < half:
                    there = slice(jx * tok, (jx + 1) * tok)
                    if jy:
                        send_a[jy - 1, there, to] = block.astype(jnp.bfloat16)
                    else:
                        keep_a[there, to] = block
                else:
                    there = slice(jy * tok, (jy + 1) * tok)
                    if jx:
                        send_b[jx - 1, there, to] = block.astype(jnp.bfloat16)
                    else:
                        keep_b[there, to] = block


def ffn(first, near, left, right, weights, place, experts, per_group):
    ny, nx = len(left) + 1, len(right) + 1
    tok, width = first.shape
    units, depth = weights[0].shape
    half, count = depth // 2, ny * nx * tok
    any_spec, vmem = pl.BlockSpec(memory_space=pl.ANY), pl.BlockSpec(memory_space=pltpu.VMEM)
    sources = [first, *near, *left, *right]
    macs = count * depth * units * 6
    return pl.pallas_call(
        functools.partial(ffn_kernel, ny, nx, experts, per_group),
        in_specs=[pl.BlockSpec(memory_space=pltpu.SMEM)] + [any_spec] * len(sources) + [vmem] * 6,
        out_specs=[vmem] * 4,
        out_shape=[
            jax.ShapeDtypeStruct((ny - 1, nx * tok, half), jnp.bfloat16),
            jax.ShapeDtypeStruct((nx * tok, half), jnp.float32),
            jax.ShapeDtypeStruct((nx - 1, ny * tok, half), jnp.bfloat16),
            jax.ShapeDtypeStruct((ny * tok, half), jnp.float32),
        ],
        scratch_shapes=[
            pltpu.VMEM((count, width), jnp.bfloat16),
            pltpu.VMEM((2, count, units), jnp.bfloat16),
            pltpu.SemaphoreType.DMA((2 * ny * nx,)),
        ],
        compiler_params=pltpu.CompilerParams(vmem_limit_bytes=14 * 1024 * 1024),
        cost_estimate=pl.CostEstimate(
            flops=macs // 1000,
            bytes_accessed=count,
            transcendentals=0,
        ),
    )(place, *sources, *weights)


def shift(value, axis, by):
    n = lax.axis_size(axis)
    return lax.ppermute(value, axis, [(i, (i + by) % n) for i in range(n)])


def ring_step(value):
    n = lax.axis_size("line")
    order = list(range(1, n, 2)) + list(range(0, n, 2))[::-1]
    return lax.ppermute(value, "line", [(order[i], order[(i + 1) % n]) for i in range(n)])


def after(value, *earlier):
    return lax.optimization_barrier((value, earlier))[0]


def per_device(tokens, expert_ids, combine, gate_weight, up_weight, down_weight):
    ny, nx, stages = lax.axis_size("e_hi"), lax.axis_size("e_lo"), lax.axis_size("line")
    per_group, units, depth = gate_weight.shape
    experts = ny * nx * per_group
    tok = tokens.shape[0]
    half = depth // 2
    split = (tok // 2 + 15) // 16 * 16
    group = lax.axis_index(("e_hi", "e_lo")).astype(jnp.int32).reshape(1)

    tokens, combine = after((tokens, combine), group)

    chosen = expert_ids[:, :, None] == jnp.arange(experts, dtype=jnp.int32)[None, None, :]
    named = jnp.sum(jnp.where(chosen, combine[:, :, None], 0.0), axis=1)
    high = named.astype(jnp.bfloat16)
    rest = (named - high.astype(jnp.float32)).astype(jnp.bfloat16)
    pad = jnp.zeros((tok, LANES * -(-2 * experts // LANES) - 2 * experts), jnp.bfloat16)
    first = jnp.concatenate([tokens, high, rest, pad], axis=1)

    def add(*terms):
        return sum(t.astype(jnp.float32) for t in terms)

    seen = []

    def held(value):
        return after(value, list(seen)) if seen else value

    def wait(*values):
        seen.extend(values)

    def neighbours(axis, pieces, sign=1):
        return [shift(held(p), axis, sign * j) for j, p in enumerate(pieces, 1)]

    def near_of(lefts, rights):
        if nx == ny:
            return [jnp.concatenate([a, b], axis=1) for a, b in zip(lefts, rights)]
        return lefts + rights

    def halves_of(near):
        if nx == ny:
            return [n[:, :half] for n in near], [n[:, half:] for n in near]
        return near[: nx - 1], near[nx - 1 :]

    def opened(slot):
        slot = held(slot)
        if len(slot) > 1:
            return slot[0], slot[1:]
        n = slot[0].shape[0] // nx
        return slot[0][:n], [slot[0][i * n : (i + 1) * n] for i in range(1, nx)]

    def along(slot, low, high):
        first, near = opened(slot)
        arrays = [a[low:high] for a in [first, *near]]
        if nx == ny:
            arrays = [jnp.concatenate(arrays)]
        return [ring_step(a) for a in arrays]

    def to_y(slot):
        first, near = opened(slot)
        left = jnp.concatenate([first[:, :half], *halves_of(near)[0]])
        return [shift(left, "e_hi", j) for j in range(1, ny)]

    def to_x(slot):
        first, near = opened(slot)
        right = jnp.concatenate([first[:, half:], *halves_of(near)[1]])
        return [shift(right, "e_lo", j) for j in range(1, nx)]

    def exchange(slot):
        return to_y(slot), to_x(slot)

    def run(slot, sides):
        first, near = opened(slot)
        if nx == ny:
            lefts, rights = halves_of(near)
            near = lefts + rights
        parts = ffn(first, near, *held(sides), weights, group, experts, per_group)
        seen[:] = [parts]
        return parts

    def start_sums(parts):
        send_a, keep_a, send_b, keep_b = parts
        got_a = neighbours("e_hi", [send_a[j] for j in range(ny - 1)], -1)
        got_b = neighbours("e_lo", [send_b[j] for j in range(nx - 1)], -1)
        return [keep_a] + got_a, [keep_b] + got_b

    def finish_sums(terms):
        terms_a, terms_b = held(terms)
        sum_a = add(*terms_a).reshape(nx, -1, half)
        sum_b = add(*terms_b).reshape(ny, -1, half)
        last_a = [shift(sum_a[j].astype(jnp.bfloat16), "e_lo", -j) for j in range(1, nx)]
        last_b = [shift(sum_b[j].astype(jnp.bfloat16), "e_hi", -j) for j in range(1, ny)]
        return [sum_a[0]] + last_a, [sum_b[0]] + last_b

    def pass_on(terms):
        terms_a, terms_b = held(terms)
        sums = add(*terms_a), add(*terms_b)
        sums = ring_step(jnp.concatenate(sums, axis=1 if nx == ny else 0).astype(jnp.bfloat16))
        if nx == ny:
            return [sums[:, :half]], [sums[:, half:]]
        return [sums[: nx * tok]], [sums[nx * tok :]]

    def with_terms(terms, more):
        return terms[0] + more[0], terms[1] + more[1]

    def joined(low, high):
        def rows(part, count):
            return [t.reshape(count, -1, half) for t in part]

        sides = []
        for part_low, part_high, count in ((low[0], high[0], nx), (low[1], high[1], ny)):
            both = zip(rows(part_low, count), rows(part_high, count))
            sides.append([jnp.concatenate(b, axis=1).reshape(-1, half) for b in both])
        return sides

    def total_of(ended, *carry):
        ended, carry = held((ended, carry))
        a = add(*ended[0], *[c[:, :half] for c in carry])
        b = add(*ended[1], *[c[:, half:] for c in carry])
        return jnp.concatenate([a, b], axis=1).astype(jnp.bfloat16)

    own = [w.reshape(per_group * units, depth) for w in (gate_weight, up_weight, down_weight)]
    lefts = neighbours("e_lo", [tokens[:, :half]] * (nx - 1))
    next_first = ring_step(first)
    rights = neighbours("e_hi", [first[:, half:]] * (ny - 1))
    other = [shift(w, "core", 1) for w in own[:2]]
    near = near_of(lefts, rights)
    slot = [[first, *near]]
    wait(near)
    sides = [exchange(slot[0])]
    wait(next_first, other)
    next_near = [ring_step(held(n)) for n in near]
    other.append(shift(held(own[2]), "core", 1))
    wait(sides[0], next_near)
    weights = own + other
    slot.append([next_first, *next_near])
    begun, ended = {}, {}
    last = stages - 1

    for k in range(1, last):
        if k + 1 < last:
            slot.append(along(slot[k], 0, tok))
        else:
            low = along(slot[k], 0, split)
        sides.append(exchange(slot[k]))
        if k == 1:
            wait(other)
        parts = run(slot[k - 1], sides[k - 1])
        if k > 1:
            wait(begun[k - 2])
        if k + 1 == last:
            high = along(slot[k], split, tok)
            wait(low)
            low_sides = exchange(low)
        wait(sides[k])
        begun[k - 1] = start_sums(parts)
        if k + 1 < last:
            wait(slot[k + 1])
    parts = run(slot[last - 1], sides[last - 1])
    wait(high, low_sides)
    high_sides = exchange(high)
    wait(begun[last - 2])
    on_way = pass_on(begun[1])
    begun[last - 1] = start_sums(parts)
    parts = run(low, low_sides)
    wait(high_sides)
    low_sums = start_sums(parts)
    parts = run(high, high_sides)
    wait(begun[last - 1], on_way)
    ended = finish_sums(with_terms(begun[2], on_way))
    for k in range(3, last):
        wait(ended)
        moved = ring_step(total_of(ended))
        wait(moved)
        ended = finish_sums(begun[k])
        ended[0].append(moved[:, :half])
        ended[1].append(moved[:, half:])
    wait(low_sums)
    high_sums = start_sums(parts)
    wait(ended)
    carry = ring_step(total_of(ended))
    wait(high_sums)
    ends = finish_sums(joined(low_sums, high_sums))
    wait(carry, ends)
    carry = ring_step(total_of(ends, carry))
    ended = finish_sums(begun[0])
    return total_of(ended, carry)


def solution(mesh):
    groups, shards = mesh.shape["expert"], mesh.shape["fsdp"]
    split = Mesh(mesh.devices.reshape(groups // 2, 2, shards // 2, 2), AXES)
    whole, expert, shard = P(AXES, None), ("e_hi", "e_lo"), ("line", "core")
    return jax.shard_map(
        per_device,
        mesh=split,
        in_specs=(whole, whole, whole) + (P(expert, shard, None),) * 3,
        out_specs=whole,
        check_vma=False,
    )
```

```python
import functools

import jax
import jax.numpy as jnp
from jax import lax
from jax.experimental import pallas as pl
from jax.experimental.pallas import tpu as pltpu
from jax.sharding import Mesh, PartitionSpec as P

AXES = ("e_hi", "e_lo", "line", "core")
LANES = 128
TILE = 256


def tiles(extent, size=TILE):
    return [(at, min(size, extent - at)) for at in range(0, extent, size)]


def ffn_kernel(ny, nx, experts, per_group, *refs):
    first, refs = refs[0], refs[1:]
    near, refs = refs[: nx + ny - 2], refs[nx + ny - 2 :]
    left, right, refs = refs[: ny - 1], refs[ny - 1 : ny + nx - 2], refs[ny + nx - 2 :]
    weights, refs = refs[:6], refs[6:]
    send_a, keep_a, send_b, keep_b = refs[:4]
    rows, hidden, row_sem = refs[4:]
    count, depth = rows.shape[0], weights[0].shape[1]
    half = depth // 2
    units = weights[0].shape[0]
    tok = count // (ny * nx)
    group = lax.axis_index("e_hi") * nx + lax.axis_index("e_lo")

    row_copies = []

    def bring(source, from_row, block, low):
        cols = pl.ds(0, half) if low else pl.ds(half, rows.shape[1] - half)
        from_cols = cols if source.shape[1] == rows.shape[1] else pl.ds(0, source.shape[1])
        row_copies.append(
            pltpu.make_async_copy(
                source.at[pl.ds(from_row, tok), from_cols],
                rows.at[pl.ds(block * tok, tok), cols],
                row_sem.at[len(row_copies)],
            )
        )

    for jy in range(ny):
        for jx in range(nx):
            block = jy * nx + jx
            if jy:
                bring(left[jy - 1], jx * tok, block, True)
            else:
                bring(near[jx - 1] if jx else first, 0, block, True)
            if jx:
                bring(right[jx - 1], jy * tok, block, False)
            else:
                bring(near[nx - 1 + jy - 1] if jy else first, 0, block, False)
    for copy in row_copies:
        copy.start()
    for copy in row_copies:
        copy.wait()

    extra = rows[:, depth:].astype(jnp.float32)
    lane = lax.broadcasted_iota(jnp.int32, extra.shape, 1)
    named = []
    for e in range(per_group):
        mine = group * per_group + e
        pick = (lane == mine) | (lane == mine + experts)
        named.append(0.5 * jnp.sum(jnp.where(pick, extra, 0.0), axis=1, keepdims=True))

    per_expert = units // per_group
    nt = (((1,), (1,)), ((), ()))
    for h in range(2):
        gate, up = weights[3 * h], weights[3 * h + 1]
        for start, size in tiles(units):
            gate_pre = lax.dot_general(
                rows[:, :depth],
                gate[start : start + size],
                nt,
                preferred_element_type=jnp.float32,
            )
            up_pre = lax.dot_general(
                rows[:, :depth],
                up[start : start + size],
                nt,
                preferred_element_type=jnp.float32,
            )
            low, high = start // per_expert, (start + size - 1) // per_expert
            column = lax.broadcasted_iota(jnp.int32, (1, size), 1) + start
            scale = named[high]
            for e in range(high - 1, low - 1, -1):
                scale = jnp.where(column < (e + 1) * per_expert, named[e], scale)
            value = gate_pre * (1.0 + jnp.tanh(0.5 * gate_pre)) * (up_pre * scale)
            hidden[h, :, start : start + size] = value.astype(jnp.bfloat16)
    for start, size in tiles(depth):
        part = sum(
            jnp.dot(
                hidden[h],
                weights[3 * h + 2][:, start : start + size],
                preferred_element_type=jnp.float32,
            )
            for h in range(2)
        )
        to = slice(start % half, start % half + size)
        for jy in range(ny):
            for jx in range(nx):
                at = (jy * nx + jx) * tok
                block = part[at : at + tok]
                if start < half:
                    there = slice(jx * tok, (jx + 1) * tok)
                    if jy:
                        send_a[jy - 1, there, to] = block.astype(jnp.bfloat16)
                    else:
                        keep_a[there, to] = block
                else:
                    there = slice(jy * tok, (jy + 1) * tok)
                    if jx:
                        send_b[jx - 1, there, to] = block.astype(jnp.bfloat16)
                    else:
                        keep_b[there, to] = block


def ffn(first, near, left, right, weights, experts, per_group):
    ny, nx = len(left) + 1, len(right) + 1
    tok, width = first.shape
    units, depth = weights[0].shape
    half, count = depth // 2, ny * nx * tok
    any_spec, vmem = pl.BlockSpec(memory_space=pl.ANY), pl.BlockSpec(memory_space=pltpu.VMEM)
    sources = [first, *near, *left, *right]
    macs = count * depth * units * 6
    return pl.pallas_call(
        functools.partial(ffn_kernel, ny, nx, experts, per_group),
        in_specs=[any_spec] * len(sources) + [vmem] * 6,
        out_specs=[vmem] * 4,
        out_shape=[
            jax.ShapeDtypeStruct((ny - 1, nx * tok, half), jnp.bfloat16),
            jax.ShapeDtypeStruct((nx * tok, half), jnp.float32),
            jax.ShapeDtypeStruct((nx - 1, ny * tok, half), jnp.bfloat16),
            jax.ShapeDtypeStruct((ny * tok, half), jnp.float32),
        ],
        scratch_shapes=[
            pltpu.VMEM((count, width), jnp.bfloat16),
            pltpu.VMEM((2, count, units), jnp.bfloat16),
            pltpu.SemaphoreType.DMA((2 * ny * nx,)),
        ],
        compiler_params=pltpu.CompilerParams(vmem_limit_bytes=14 * 1024 * 1024),
        cost_estimate=pl.CostEstimate(
            flops=2 * macs,
            bytes_accessed=8 * count * depth,
            transcendentals=2 * count * units,
        ),
    )(*sources, *weights)


def shift(value, axis, by):
    n = lax.axis_size(axis)
    return lax.ppermute(value, axis, [(i, (i + by) % n) for i in range(n)])


def ring_step(value):
    n = lax.axis_size("line")
    order = list(range(1, n, 2)) + list(range(0, n, 2))[::-1]
    return lax.ppermute(value, "line", [(order[i], order[(i + 1) % n]) for i in range(n)])


def after(value, *earlier):
    return lax.optimization_barrier((value, earlier))[0]


def per_device(tokens, expert_ids, combine, gate_weight, up_weight, down_weight):
    ny, nx, stages = lax.axis_size("e_hi"), lax.axis_size("e_lo"), lax.axis_size("line")
    per_group, units, depth = gate_weight.shape
    experts = ny * nx * per_group
    tok = tokens.shape[0]
    half = depth // 2

    chosen = expert_ids[:, :, None] == jnp.arange(experts, dtype=jnp.int32)[None, None, :]
    named = jnp.sum(jnp.where(chosen, combine[:, :, None], 0.0), axis=1)
    high = named.astype(jnp.bfloat16)
    rest = (named - high.astype(jnp.float32)).astype(jnp.bfloat16)
    pad = jnp.zeros((tok, LANES * -(-2 * experts // LANES) - 2 * experts), jnp.bfloat16)
    first = jnp.concatenate([tokens, high, rest, pad], axis=1)

    def near_of(pieces):
        if nx == ny:
            lefts, rights = pieces[: nx - 1], pieces[nx - 1 :]
            return [jnp.concatenate([a, b], axis=1) for a, b in zip(lefts, rights)]
        return pieces

    def halves_of(near):
        if nx == ny:
            return [n[:, :half] for n in near], [n[:, half:] for n in near]
        return near[: nx - 1], near[nx - 1 :]

    near = [shift(tokens[:, :half], "e_lo", j) for j in range(1, nx)]
    near += [shift(first[:, half:], "e_hi", j) for j in range(1, ny)]
    near = near_of(near)

    own = [w.reshape(per_group * units, depth) for w in (gate_weight, up_weight, down_weight)]
    other = [shift(own[0], "core", 1)]

    def add(*terms):
        return sum(t.astype(jnp.float32) for t in terms)

    def exchange(first, near):
        lefts, rights = halves_of(near)
        left = jnp.concatenate([first[:, :half], *lefts])
        right = jnp.concatenate([first[:, half:], *rights])
        return (
            [shift(left, "e_hi", j) for j in range(1, ny)],
            [shift(right, "e_lo", j) for j in range(1, nx)],
        )

    def run(first, near, sides, *earlier):
        first, sides = after((first, sides), *earlier)
        if nx == ny:
            lefts, rights = halves_of(near)
            near = lefts + rights
        return ffn(first, near, *sides, weights, experts, per_group)

    def start_sums(parts, *earlier):
        send_a, keep_a, send_b, keep_b = parts
        send_a, send_b = after((send_a, send_b), *earlier)
        got_a = [shift(send_a[j - 1], "e_hi", -j) for j in range(1, ny)]
        got_b = [shift(send_b[j - 1], "e_lo", -j) for j in range(1, nx)]
        return [keep_a] + got_a, [keep_b] + got_b

    def finish_sums(terms_a, terms_b):
        sum_a = add(*terms_a).reshape(nx, tok, half)
        sum_b = add(*terms_b).reshape(ny, tok, half)
        last_a = [shift(sum_a[j].astype(jnp.bfloat16), "e_lo", -j) for j in range(1, nx)]
        last_b = [shift(sum_b[j].astype(jnp.bfloat16), "e_hi", -j) for j in range(1, ny)]
        return [sum_a[0]] + last_a, [sum_b[0]] + last_b

    firsts, nears, sides = [first], [near], [exchange(first, near)]
    firsts.append(ring_step(first))
    nears.append([ring_step(n) for n in near])
    other.append(shift(after(own[1], other[0], near, firsts[1]), "core", 1))
    other.append(shift(after(own[2], other[0], near, firsts[1]), "core", 1))
    weights = own + other

    parts, begun = {}, {}
    for k in range(1, stages):
        sides.append(exchange(firsts[k], nears[k]))
        if k + 1 < stages:
            if nx == ny:
                pair = jnp.concatenate([firsts[k], *nears[k]])
                pair = ring_step(pair)
                firsts.append(pair[:tok])
                nears.append([pair[i * tok : (i + 1) * tok] for i in range(1, nx)])
            else:
                firsts.append(ring_step(firsts[k]))
                nears.append([ring_step(n) for n in nears[k]])
        earlier = firsts[k], nears[k], begun.get(k - 2)
        parts[k - 1] = run(firsts[k - 1], nears[k - 1], sides[k - 1], *earlier)
        begun[k - 1] = start_sums(parts[k - 1], sides[k])
    last = stages - 1
    parts[last] = run(
        firsts[last], nears[last], sides[last], parts[last - 1], begun[last - 2]
    )
    begun[last] = start_sums(parts[last], begun[last - 1])

    carry_a, carry_b = [], []
    for k in list(range(1, stages)) + [0]:
        terms_a, terms_b = begun[k]
        if k == 1:
            sums = jnp.concatenate([add(*terms_a), add(*terms_b)], axis=1 if nx == ny else 0)
            sums = ring_step(sums.astype(jnp.bfloat16))
            if nx == ny:
                mid_a, mid_b = [sums[:, :half]], [sums[:, half:]]
            else:
                mid_a, mid_b = [sums[: nx * tok]], [sums[nx * tok :]]
            continue
        if k == 0:
            mid_a, mid_b = [], []
        a, b = finish_sums(terms_a + mid_a, terms_b + mid_b)
        mid_a, mid_b = [], []
        total = jnp.concatenate([add(*a, *carry_a), add(*b, *carry_b)], axis=1)
        total = total.astype(jnp.bfloat16)
        if k:
            total = ring_step(total)
            carry_a, carry_b = [total[:, :half]], [total[:, half:]]
    return total


def solution(mesh):
    groups, shards = mesh.shape["expert"], mesh.shape["fsdp"]
    split = Mesh(mesh.devices.reshape(groups // 2, 2, shards // 2, 2), AXES)
    whole, expert, shard = P(AXES, None), ("e_hi", "e_lo"), ("line", "core")
    return jax.shard_map(
        per_device,
        mesh=split,
        in_specs=(whole, whole, whole) + (P(expert, shard, None),) * 3,
        out_specs=whole,
        check_vma=False,
    )
```

```python
import functools

import jax
import jax.numpy as jnp
from jax import lax
from jax.experimental import pallas as pl
from jax.experimental.pallas import tpu as pltpu
from jax.sharding import Mesh, PartitionSpec as P

AXES = ("e_hi", "e_lo", "line", "core")
LANES = 128
TILE = 256


def tiles(extent, size=TILE):
    return [(at, min(size, extent - at)) for at in range(0, extent, size)]


def ffn_kernel(ny, nx, experts, per_group, *refs):
    first, refs = refs[0], refs[1:]
    near, refs = refs[: nx + ny - 2], refs[nx + ny - 2 :]
    left, right, refs = refs[: ny - 1], refs[ny - 1 : ny + nx - 2], refs[ny + nx - 2 :]
    weights, refs = refs[:6], refs[6:]
    send_a, keep_a, send_b, keep_b = refs[:4]
    rows, hidden, row_sem = refs[4:]
    count, depth = rows.shape[0], weights[0].shape[1]
    half = depth // 2
    units = weights[0].shape[0]
    tok = count // (ny * nx)
    group = lax.axis_index("e_hi") * nx + lax.axis_index("e_lo")

    row_copies = []

    def bring(source, from_row, block, low):
        cols = pl.ds(0, half) if low else pl.ds(half, rows.shape[1] - half)
        from_cols = cols if source.shape[1] == rows.shape[1] else pl.ds(0, source.shape[1])
        row_copies.append(
            pltpu.make_async_copy(
                source.at[pl.ds(from_row, tok), from_cols],
                rows.at[pl.ds(block * tok, tok), cols],
                row_sem.at[len(row_copies)],
            )
        )

    for jy in range(ny):
        for jx in range(nx):
            block = jy * nx + jx
            if jy:
                bring(left[jy - 1], jx * tok, block, True)
            else:
                bring(near[jx - 1] if jx else first, 0, block, True)
            if jx:
                bring(right[jx - 1], jy * tok, block, False)
            else:
                bring(near[nx - 1 + jy - 1] if jy else first, 0, block, False)
    for copy in row_copies:
        copy.start()
    for copy in row_copies:
        copy.wait()

    extra = rows[:, depth:].astype(jnp.float32)
    lane = lax.broadcasted_iota(jnp.int32, extra.shape, 1)
    named = []
    for e in range(per_group):
        mine = group * per_group + e
        pick = (lane == mine) | (lane == mine + experts)
        named.append(0.5 * jnp.sum(jnp.where(pick, extra, 0.0), axis=1, keepdims=True))

    per_expert = units // per_group
    nt = (((1,), (1,)), ((), ()))
    for h in range(2):
        gate, up = weights[3 * h], weights[3 * h + 1]
        for start, size in tiles(units):
            gate_pre = lax.dot_general(
                rows[:, :depth],
                gate[start : start + size],
                nt,
                preferred_element_type=jnp.float32,
            )
            up_pre = lax.dot_general(
                rows[:, :depth],
                up[start : start + size],
                nt,
                preferred_element_type=jnp.float32,
            )
            low, high = start // per_expert, (start + size - 1) // per_expert
            column = lax.broadcasted_iota(jnp.int32, (1, size), 1) + start
            scale = named[high]
            for e in range(high - 1, low - 1, -1):
                scale = jnp.where(column < (e + 1) * per_expert, named[e], scale)
            value = gate_pre * (1.0 + jnp.tanh(0.5 * gate_pre)) * (up_pre * scale)
            hidden[h, :, start : start + size] = value.astype(jnp.bfloat16)
    for start, size in tiles(depth):
        part = sum(
            jnp.dot(
                hidden[h],
                weights[3 * h + 2][:, start : start + size],
                preferred_element_type=jnp.float32,
            )
            for h in range(2)
        )
        to = slice(start % half, start % half + size)
        for jy in range(ny):
            for jx in range(nx):
                at = (jy * nx + jx) * tok
                block = part[at : at + tok]
                if start < half:
                    there = slice(jx * tok, (jx + 1) * tok)
                    if jy:
                        send_a[jy - 1, there, to] = block.astype(jnp.bfloat16)
                    else:
                        keep_a[there, to] = block
                else:
                    there = slice(jy * tok, (jy + 1) * tok)
                    if jx:
                        send_b[jx - 1, there, to] = block.astype(jnp.bfloat16)
                    else:
                        keep_b[there, to] = block


def ffn(first, near, left, right, weights, experts, per_group):
    ny, nx = len(left) + 1, len(right) + 1
    tok, width = first.shape
    units, depth = weights[0].shape
    half, count = depth // 2, ny * nx * tok
    any_spec, vmem = pl.BlockSpec(memory_space=pl.ANY), pl.BlockSpec(memory_space=pltpu.VMEM)
    sources = [first, *near, *left, *right]
    macs = count * depth * units * 6
    return pl.pallas_call(
        functools.partial(ffn_kernel, ny, nx, experts, per_group),
        in_specs=[any_spec] * len(sources) + [vmem] * 6,
        out_specs=[vmem] * 4,
        out_shape=[
            jax.ShapeDtypeStruct((ny - 1, nx * tok, half), jnp.bfloat16),
            jax.ShapeDtypeStruct((nx * tok, half), jnp.float32),
            jax.ShapeDtypeStruct((nx - 1, ny * tok, half), jnp.bfloat16),
            jax.ShapeDtypeStruct((ny * tok, half), jnp.float32),
        ],
        scratch_shapes=[
            pltpu.VMEM((count, width), jnp.bfloat16),
            pltpu.VMEM((2, count, units), jnp.bfloat16),
            pltpu.SemaphoreType.DMA((2 * ny * nx,)),
        ],
        compiler_params=pltpu.CompilerParams(vmem_limit_bytes=14 * 1024 * 1024),
        cost_estimate=pl.CostEstimate(
            flops=macs // 1000,
            bytes_accessed=count,
            transcendentals=0,
        ),
    )(*sources, *weights)


def shift(value, axis, by):
    n = lax.axis_size(axis)
    return lax.ppermute(value, axis, [(i, (i + by) % n) for i in range(n)])


def ring_step(value):
    n = lax.axis_size("line")
    order = list(range(1, n, 2)) + list(range(0, n, 2))[::-1]
    return lax.ppermute(value, "line", [(order[i], order[(i + 1) % n]) for i in range(n)])


def after(value, *earlier):
    return lax.optimization_barrier((value, earlier))[0]


def per_device(tokens, expert_ids, combine, gate_weight, up_weight, down_weight):
    ny, nx, stages = lax.axis_size("e_hi"), lax.axis_size("e_lo"), lax.axis_size("line")
    per_group, units, depth = gate_weight.shape
    experts = ny * nx * per_group
    tok = tokens.shape[0]
    half = depth // 2
    split = (tok // 2 + 15) // 16 * 16

    chosen = expert_ids[:, :, None] == jnp.arange(experts, dtype=jnp.int32)[None, None, :]
    named = jnp.sum(jnp.where(chosen, combine[:, :, None], 0.0), axis=1)
    high = named.astype(jnp.bfloat16)
    rest = (named - high.astype(jnp.float32)).astype(jnp.bfloat16)
    pad = jnp.zeros((tok, LANES * -(-2 * experts // LANES) - 2 * experts), jnp.bfloat16)
    first = jnp.concatenate([tokens, high, rest, pad], axis=1)

    def add(*terms):
        return sum(t.astype(jnp.float32) for t in terms)

    seen = []

    def held(value):
        return after(value, list(seen)) if seen else value

    def wait(*values):
        seen.extend(values)

    def neighbours(axis, pieces, sign=1):
        return [shift(held(p), axis, sign * j) for j, p in enumerate(pieces, 1)]

    def near_of(lefts, rights):
        if nx == ny:
            return [jnp.concatenate([a, b], axis=1) for a, b in zip(lefts, rights)]
        return lefts + rights

    def halves_of(near):
        if nx == ny:
            return [n[:, :half] for n in near], [n[:, half:] for n in near]
        return near[: nx - 1], near[nx - 1 :]

    def opened(slot):
        slot = held(slot)
        if len(slot) > 1:
            return slot[0], slot[1:]
        n = slot[0].shape[0] // nx
        return slot[0][:n], [slot[0][i * n : (i + 1) * n] for i in range(1, nx)]

    def along(slot, low, high):
        first, near = opened(slot)
        arrays = [a[low:high] for a in [first, *near]]
        if nx == ny:
            arrays = [jnp.concatenate(arrays)]
        return [ring_step(a) for a in arrays]

    def to_y(slot):
        first, near = opened(slot)
        left = jnp.concatenate([first[:, :half], *halves_of(near)[0]])
        return [shift(left, "e_hi", j) for j in range(1, ny)]

    def to_x(slot):
        first, near = opened(slot)
        right = jnp.concatenate([first[:, half:], *halves_of(near)[1]])
        return [shift(right, "e_lo", j) for j in range(1, nx)]

    def exchange(slot):
        return to_y(slot), to_x(slot)

    def run(slot, sides):
        first, near = opened(slot)
        if nx == ny:
            lefts, rights = halves_of(near)
            near = lefts + rights
        parts = ffn(first, near, *held(sides), weights, experts, per_group)
        seen[:] = [parts]
        return parts

    def start_sums(parts):
        send_a, keep_a, send_b, keep_b = parts
        got_a = neighbours("e_hi", [send_a[j] for j in range(ny - 1)], -1)
        got_b = neighbours("e_lo", [send_b[j] for j in range(nx - 1)], -1)
        return [keep_a] + got_a, [keep_b] + got_b

    def finish_sums(terms):
        terms_a, terms_b = held(terms)
        sum_a = add(*terms_a).reshape(nx, -1, half)
        sum_b = add(*terms_b).reshape(ny, -1, half)
        last_a = [shift(sum_a[j].astype(jnp.bfloat16), "e_lo", -j) for j in range(1, nx)]
        last_b = [shift(sum_b[j].astype(jnp.bfloat16), "e_hi", -j) for j in range(1, ny)]
        return [sum_a[0]] + last_a, [sum_b[0]] + last_b

    def pass_on(terms):
        terms_a, terms_b = held(terms)
        sums = add(*terms_a), add(*terms_b)
        sums = ring_step(jnp.concatenate(sums, axis=1 if nx == ny else 0).astype(jnp.bfloat16))
        if nx == ny:
            return [sums[:, :half]], [sums[:, half:]]
        return [sums[: nx * tok]], [sums[nx * tok :]]

    def with_terms(terms, more):
        return terms[0] + more[0], terms[1] + more[1]

    def joined(low, high):
        def rows(part, count):
            return [t.reshape(count, -1, half) for t in part]

        sides = []
        for part_low, part_high, count in ((low[0], high[0], nx), (low[1], high[1], ny)):
            both = zip(rows(part_low, count), rows(part_high, count))
            sides.append([jnp.concatenate(b, axis=1).reshape(-1, half) for b in both])
        return sides

    def total_of(ended, *carry):
        ended, carry = held((ended, carry))
        a = add(*ended[0], *[c[:, :half] for c in carry])
        b = add(*ended[1], *[c[:, half:] for c in carry])
        return jnp.concatenate([a, b], axis=1).astype(jnp.bfloat16)

    own = [w.reshape(per_group * units, depth) for w in (gate_weight, up_weight, down_weight)]
    lefts = neighbours("e_lo", [tokens[:, :half]] * (nx - 1))
    next_first = ring_step(first)
    rights = neighbours("e_hi", [first[:, half:]] * (ny - 1))
    other = [shift(w, "core", 1) for w in own[:2]]
    near = near_of(lefts, rights)
    slot = [[first, *near]]
    sides = [exchange(slot[0])]
    wait(near)
    next_near = [ring_step(held(n)) for n in near]
    wait(next_first, other[0])
    other.append(shift(held(own[2]), "core", 1))
    wait(next_near, sides[0], other)
    weights = own + other
    slot.append([next_first, *next_near])
    begun, ended = {}, {}
    last = stages - 1

    for k in range(1, last):
        if k + 1 < last:
            sides.append(exchange(slot[k]))
            slot.append(along(slot[k], 0, tok))
        else:
            low = along(slot[k], 0, split)
            sides.append(exchange(slot[k]))
        parts = run(slot[k - 1], sides[k - 1])
        if k > 1:
            wait(begun[k - 2])
        if k + 1 == last:
            high = along(slot[k], split, tok)
            low_sides = exchange(low)
        wait(sides[k])
        begun[k - 1] = start_sums(parts)
        if k + 1 < last:
            wait(slot[k + 1])
    parts = run(slot[last - 1], sides[last - 1])
    wait(high, low_sides)
    high_sides = exchange(high)
    wait(begun[last - 2])
    on_way = pass_on(begun[1])
    begun[last - 1] = start_sums(parts)
    parts = run(low, low_sides)
    wait(high_sides)
    low_sums = start_sums(parts)
    parts = run(high, high_sides)
    wait(on_way)
    ended = finish_sums(with_terms(begun[2], on_way))
    for k in range(3, last):
        wait(ended)
        moved = ring_step(total_of(ended))
        wait(moved)
        ended = finish_sums(begun[k])
        ended[0].append(moved[:, :half])
        ended[1].append(moved[:, half:])
    wait(low_sums, ended)
    carry = ring_step(total_of(ended))
    high_sums = start_sums(parts)
    ends = finish_sums(joined(low_sums, high_sums))
    wait(carry)
    carry = ring_step(total_of(ends, carry))
    ended = finish_sums(begun[0])
    return total_of(ended, carry)


def solution(mesh):
    groups, shards = mesh.shape["expert"], mesh.shape["fsdp"]
    split = Mesh(mesh.devices.reshape(groups // 2, 2, shards // 2, 2), AXES)
    whole, expert, shard = P(AXES, None), ("e_hi", "e_lo"), ("line", "core")
    return jax.shard_map(
        per_device,
        mesh=split,
        in_specs=(whole, whole, whole) + (P(expert, shard, None),) * 3,
        out_specs=whole,
        check_vma=False,
    )
```

```python
import functools

import jax
import jax.numpy as jnp
from jax import lax
from jax.experimental import pallas as pl
from jax.experimental.pallas import tpu as pltpu
from jax.sharding import Mesh, PartitionSpec as P

AXES = ("e_hi", "e_lo", "line", "core")
LANES = 128
TILE = 256


def tiles(extent, size=TILE):
    return [(at, min(size, extent - at)) for at in range(0, extent, size)]


def ffn_kernel(ny, nx, experts, per_group, *refs):
    first, refs = refs[0], refs[1:]
    near, refs = refs[: nx + ny - 2], refs[nx + ny - 2 :]
    left, right, refs = refs[: ny - 1], refs[ny - 1 : ny + nx - 2], refs[ny + nx - 2 :]
    weights, refs = refs[:6], refs[6:]
    send_a, keep_a, send_b, keep_b = refs[:4]
    rows, hidden, row_sem = refs[4:]
    count, depth = rows.shape[0], weights[0].shape[1]
    half = depth // 2
    units = weights[0].shape[0]
    tok = count // (ny * nx)
    group = lax.axis_index("e_hi") * nx + lax.axis_index("e_lo")

    row_copies = []

    def bring(source, from_row, block, low):
        cols = pl.ds(0, half) if low else pl.ds(half, rows.shape[1] - half)
        from_cols = cols if source.shape[1] == rows.shape[1] else pl.ds(0, source.shape[1])
        row_copies.append(
            pltpu.make_async_copy(
                source.at[pl.ds(from_row, tok), from_cols],
                rows.at[pl.ds(block * tok, tok), cols],
                row_sem.at[len(row_copies)],
            )
        )

    for jy in range(ny):
        for jx in range(nx):
            block = jy * nx + jx
            if jy:
                bring(left[jy - 1], jx * tok, block, True)
            else:
                bring(near[jx - 1] if jx else first, 0, block, True)
            if jx:
                bring(right[jx - 1], jy * tok, block, False)
            else:
                bring(near[nx - 1 + jy - 1] if jy else first, 0, block, False)
    for copy in row_copies:
        copy.start()
    for copy in row_copies:
        copy.wait()

    extra = rows[:, depth:].astype(jnp.float32)
    lane = lax.broadcasted_iota(jnp.int32, extra.shape, 1)
    named = []
    for e in range(per_group):
        mine = group * per_group + e
        pick = (lane == mine) | (lane == mine + experts)
        named.append(0.5 * jnp.sum(jnp.where(pick, extra, 0.0), axis=1, keepdims=True))

    per_expert = units // per_group
    nt = (((1,), (1,)), ((), ()))
    for h in range(2):
        gate, up = weights[3 * h], weights[3 * h + 1]
        for start, size in tiles(units):
            gate_pre = lax.dot_general(
                rows[:, :depth],
                gate[start : start + size],
                nt,
                preferred_element_type=jnp.float32,
            )
            up_pre = lax.dot_general(
                rows[:, :depth],
                up[start : start + size],
                nt,
                preferred_element_type=jnp.float32,
            )
            low, high = start // per_expert, (start + size - 1) // per_expert
            column = lax.broadcasted_iota(jnp.int32, (1, size), 1) + start
            scale = named[high]
            for e in range(high - 1, low - 1, -1):
                scale = jnp.where(column < (e + 1) * per_expert, named[e], scale)
            value = gate_pre * (1.0 + jnp.tanh(0.5 * gate_pre)) * (up_pre * scale)
            hidden[h, :, start : start + size] = value.astype(jnp.bfloat16)

    def down_product(start):
        cols = pl.ds(pl.multiple_of(start, TILE), TILE)
        return sum(
            jnp.dot(hidden[h], weights[3 * h + 2][:, cols], preferred_element_type=jnp.float32)
            for h in range(2)
        )

    @pl.loop(0, half // TILE)
    def _(step):
        part = down_product(step * TILE)
        to = pl.ds(pl.multiple_of(step * TILE, TILE), TILE)
        for jy in range(ny):
            block = part[jy * nx * tok : (jy + 1) * nx * tok]
            if jy:
                send_a[jy - 1, :, to] = block.astype(jnp.bfloat16)
            else:
                keep_a[:, to] = block

    @pl.loop(0, half // TILE)
    def _(step):
        part = down_product(half + step * TILE)
        to = pl.ds(pl.multiple_of(step * TILE, TILE), TILE)
        for jy in range(ny):
            for jx in range(nx):
                at = (jy * nx + jx) * tok
                block = part[at : at + tok]
                there = slice(jy * tok, (jy + 1) * tok)
                if jx:
                    send_b[jx - 1, there, to] = block.astype(jnp.bfloat16)
                else:
                    keep_b[there, to] = block


def ffn(first, near, left, right, weights, experts, per_group):
    ny, nx = len(left) + 1, len(right) + 1
    tok, width = first.shape
    units, depth = weights[0].shape
    half, count = depth // 2, ny * nx * tok
    any_spec, vmem = pl.BlockSpec(memory_space=pl.ANY), pl.BlockSpec(memory_space=pltpu.VMEM)
    sources = [first, *near, *left, *right]
    macs = count * depth * units * 6
    return pl.pallas_call(
        functools.partial(ffn_kernel, ny, nx, experts, per_group),
        in_specs=[any_spec] * len(sources) + [vmem] * 6,
        out_specs=[vmem] * 4,
        out_shape=[
            jax.ShapeDtypeStruct((ny - 1, nx * tok, half), jnp.bfloat16),
            jax.ShapeDtypeStruct((nx * tok, half), jnp.float32),
            jax.ShapeDtypeStruct((nx - 1, ny * tok, half), jnp.bfloat16),
            jax.ShapeDtypeStruct((ny * tok, half), jnp.float32),
        ],
        scratch_shapes=[
            pltpu.VMEM((count, width), jnp.bfloat16),
            pltpu.VMEM((2, count, units), jnp.bfloat16),
            pltpu.SemaphoreType.DMA((2 * ny * nx,)),
        ],
        compiler_params=pltpu.CompilerParams(vmem_limit_bytes=14 * 1024 * 1024),
        cost_estimate=pl.CostEstimate(
            flops=2 * macs,
            bytes_accessed=8 * count * depth,
            transcendentals=2 * count * units,
        ),
    )(*sources, *weights)


def shift(value, axis, by):
    n = lax.axis_size(axis)
    return lax.ppermute(value, axis, [(i, (i + by) % n) for i in range(n)])


def ring_step(value):
    n = lax.axis_size("line")
    order = list(range(1, n, 2)) + list(range(0, n, 2))[::-1]
    return lax.ppermute(value, "line", [(order[i], order[(i + 1) % n]) for i in range(n)])


def after(value, *earlier):
    return lax.optimization_barrier((value, earlier))[0]


def per_device(tokens, expert_ids, combine, gate_weight, up_weight, down_weight):
    ny, nx, stages = lax.axis_size("e_hi"), lax.axis_size("e_lo"), lax.axis_size("line")
    per_group, units, depth = gate_weight.shape
    experts = ny * nx * per_group
    tok = tokens.shape[0]
    half = depth // 2

    chosen = expert_ids[:, :, None] == jnp.arange(experts, dtype=jnp.int32)[None, None, :]
    named = jnp.sum(jnp.where(chosen, combine[:, :, None], 0.0), axis=1)
    high = named.astype(jnp.bfloat16)
    rest = (named - high.astype(jnp.float32)).astype(jnp.bfloat16)
    pad = jnp.zeros((tok, LANES * -(-2 * experts // LANES) - 2 * experts), jnp.bfloat16)
    first = jnp.concatenate([tokens, high, rest, pad], axis=1)

    def near_of(pieces):
        if nx == ny:
            lefts, rights = pieces[: nx - 1], pieces[nx - 1 :]
            return [jnp.concatenate([a, b], axis=1) for a, b in zip(lefts, rights)]
        return pieces

    def halves_of(near):
        if nx == ny:
            return [n[:, :half] for n in near], [n[:, half:] for n in near]
        return near[: nx - 1], near[nx - 1 :]

    near = [shift(tokens[:, :half], "e_lo", j) for j in range(1, nx)]
    near += [shift(first[:, half:], "e_hi", j) for j in range(1, ny)]
    near = near_of(near)

    own = [w.reshape(per_group * units, depth) for w in (gate_weight, up_weight, down_weight)]
    other = [shift(own[0], "core", 1)]

    def add(*terms):
        return sum(t.astype(jnp.float32) for t in terms)

    def exchange(first, near):
        lefts, rights = halves_of(near)
        left = jnp.concatenate([first[:, :half], *lefts])
        right = jnp.concatenate([first[:, half:], *rights])
        return (
            [shift(left, "e_hi", j) for j in range(1, ny)],
            [shift(right, "e_lo", j) for j in range(1, nx)],
        )

    def run(first, near, sides, *earlier):
        first, sides = after((first, sides), *earlier)
        if nx == ny:
            lefts, rights = halves_of(near)
            near = lefts + rights
        return ffn(first, near, *sides, weights, experts, per_group)

    def start_sums(parts, *earlier):
        send_a, keep_a, send_b, keep_b = parts
        send_a, send_b = after((send_a, send_b), *earlier)
        got_a = [shift(send_a[j - 1], "e_hi", -j) for j in range(1, ny)]
        got_b = [shift(send_b[j - 1], "e_lo", -j) for j in range(1, nx)]
        return [keep_a] + got_a, [keep_b] + got_b

    def finish_sums(terms_a, terms_b):
        sum_a = add(*terms_a).reshape(nx, tok, half)
        sum_b = add(*terms_b).reshape(ny, tok, half)
        last_a = [shift(sum_a[j].astype(jnp.bfloat16), "e_lo", -j) for j in range(1, nx)]
        last_b = [shift(sum_b[j].astype(jnp.bfloat16), "e_hi", -j) for j in range(1, ny)]
        return [sum_a[0]] + last_a, [sum_b[0]] + last_b

    firsts, nears, sides = [first], [near], [exchange(first, near)]
    firsts.append(ring_step(first))
    nears.append([ring_step(n) for n in near])
    other.append(shift(after(own[1], other[0], near, firsts[1]), "core", 1))
    other.append(shift(after(own[2], other[0], near, firsts[1]), "core", 1))
    weights = own + other

    parts, begun = {}, {}
    for k in range(1, stages):
        sides.append(exchange(firsts[k], nears[k]))
        if k + 1 < stages:
            if nx == ny:
                pair = jnp.concatenate([firsts[k], *nears[k]])
                pair = ring_step(pair)
                firsts.append(pair[:tok])
                nears.append([pair[i * tok : (i + 1) * tok] for i in range(1, nx)])
            else:
                firsts.append(ring_step(firsts[k]))
                nears.append([ring_step(n) for n in nears[k]])
        earlier = firsts[k], nears[k], begun.get(k - 2)
        parts[k - 1] = run(firsts[k - 1], nears[k - 1], sides[k - 1], *earlier)
        begun[k - 1] = start_sums(parts[k - 1], sides[k])
    last = stages - 1
    parts[last] = run(
        firsts[last], nears[last], sides[last], parts[last - 1], begun[last - 2]
    )
    begun[last] = start_sums(parts[last], begun[last - 1])

    carry_a, carry_b = [], []
    for k in list(range(1, stages)) + [0]:
        terms_a, terms_b = begun[k]
        if k == 1:
            sums = jnp.concatenate([add(*terms_a), add(*terms_b)], axis=1 if nx == ny else 0)
            sums = ring_step(sums.astype(jnp.bfloat16))
            if nx == ny:
                mid_a, mid_b = [sums[:, :half]], [sums[:, half:]]
            else:
                mid_a, mid_b = [sums[: nx * tok]], [sums[nx * tok :]]
            continue
        if k == 0:
            mid_a, mid_b = [], []
        a, b = finish_sums(terms_a + mid_a, terms_b + mid_b)
        mid_a, mid_b = [], []
        total = jnp.concatenate([add(*a, *carry_a), add(*b, *carry_b)], axis=1)
        total = total.astype(jnp.bfloat16)
        if k:
            total = ring_step(total)
            carry_a, carry_b = [total[:, :half]], [total[:, half:]]
    return total


def solution(mesh):
    groups, shards = mesh.shape["expert"], mesh.shape["fsdp"]
    split = Mesh(mesh.devices.reshape(groups // 2, 2, shards // 2, 2), AXES)
    whole, expert, shard = P(AXES, None), ("e_hi", "e_lo"), ("line", "core")
    return jax.shard_map(
        per_device,
        mesh=split,
        in_specs=(whole, whole, whole) + (P(expert, shard, None),) * 3,
        out_specs=whole,
        check_vma=False,
    )
```

```python
import functools

import jax
import jax.numpy as jnp
from jax import lax
from jax.experimental import pallas as pl
from jax.experimental.pallas import tpu as pltpu
from jax.sharding import Mesh, PartitionSpec as P

AXES = ("e_hi", "e_lo", "line", "core")
LANES = 128
TILE = 256


def tiles(extent, size=TILE):
    return [(at, min(size, extent - at)) for at in range(0, extent, size)]


def ffn_kernel(ny, nx, experts, per_group, *refs):
    first, refs = refs[0], refs[1:]
    near, refs = refs[: nx + ny - 2], refs[nx + ny - 2 :]
    left, right, refs = refs[: ny - 1], refs[ny - 1 : ny + nx - 2], refs[ny + nx - 2 :]
    weights, refs = refs[:6], refs[6:]
    send_a, keep_a, send_b, keep_b = refs[:4]
    rows, hidden, row_sem = refs[4:]
    count, depth = rows.shape[0], weights[0].shape[1]
    half = depth // 2
    units = weights[0].shape[0]
    tok = count // (ny * nx)
    group = lax.axis_index("e_hi") * nx + lax.axis_index("e_lo")

    row_copies = []

    def bring(source, from_row, block, low):
        cols = pl.ds(0, half) if low else pl.ds(half, rows.shape[1] - half)
        from_cols = cols if source.shape[1] == rows.shape[1] else pl.ds(0, source.shape[1])
        row_copies.append(
            pltpu.make_async_copy(
                source.at[pl.ds(from_row, tok), from_cols],
                rows.at[pl.ds(block * tok, tok), cols],
                row_sem.at[len(row_copies)],
            )
        )

    for jy in range(ny):
        for jx in range(nx):
            block = jy * nx + jx
            if jy:
                bring(left[jy - 1], jx * tok, block, True)
            else:
                bring(near[jx - 1] if jx else first, 0, block, True)
            if jx:
                bring(right[jx - 1], jy * tok, block, False)
            else:
                bring(near[nx - 1 + jy - 1] if jy else first, 0, block, False)
    for copy in row_copies:
        copy.start()
    for copy in row_copies:
        copy.wait()

    extra = rows[:, depth:].astype(jnp.float32)
    lane = lax.broadcasted_iota(jnp.int32, extra.shape, 1)
    named = []
    for e in range(per_group):
        mine = group * per_group + e
        pick = (lane == mine) | (lane == mine + experts)
        named.append(0.5 * jnp.sum(jnp.where(pick, extra, 0.0), axis=1, keepdims=True))

    per_expert = units // per_group
    nt = (((1,), (1,)), ((), ()))
    for h in range(2):
        gate, up = weights[3 * h], weights[3 * h + 1]
        for start, size in tiles(units):
            gate_pre = lax.dot_general(
                rows[:, :depth],
                gate[start : start + size],
                nt,
                preferred_element_type=jnp.float32,
            )
            up_pre = lax.dot_general(
                rows[:, :depth],
                up[start : start + size],
                nt,
                preferred_element_type=jnp.float32,
            )
            low, high = start // per_expert, (start + size - 1) // per_expert
            column = lax.broadcasted_iota(jnp.int32, (1, size), 1) + start
            scale = named[high]
            for e in range(high - 1, low - 1, -1):
                scale = jnp.where(column < (e + 1) * per_expert, named[e], scale)
            value = gate_pre * (1.0 + jnp.tanh(0.5 * gate_pre)) * (up_pre * scale)
            hidden[h, :, start : start + size] = value.astype(jnp.bfloat16)

    def down_product(start):
        cols = pl.ds(pl.multiple_of(start, TILE), TILE)
        return sum(
            jnp.dot(hidden[h], weights[3 * h + 2][:, cols], preferred_element_type=jnp.float32)
            for h in range(2)
        )

    @pl.loop(0, half // TILE, unroll=2)
    def _(step):
        part = down_product(step * TILE)
        to = pl.ds(pl.multiple_of(step * TILE, TILE), TILE)
        for jy in range(ny):
            block = part[jy * nx * tok : (jy + 1) * nx * tok]
            if jy:
                send_a[jy - 1, :, to] = block.astype(jnp.bfloat16)
            else:
                keep_a[:, to] = block

    @pl.loop(0, half // TILE, unroll=2)
    def _(step):
        part = down_product(half + step * TILE)
        to = pl.ds(pl.multiple_of(step * TILE, TILE), TILE)
        for jy in range(ny):
            for jx in range(nx):
                at = (jy * nx + jx) * tok
                block = part[at : at + tok]
                there = slice(jy * tok, (jy + 1) * tok)
                if jx:
                    send_b[jx - 1, there, to] = block.astype(jnp.bfloat16)
                else:
                    keep_b[there, to] = block


def ffn(first, near, left, right, weights, experts, per_group):
    ny, nx = len(left) + 1, len(right) + 1
    tok, width = first.shape
    units, depth = weights[0].shape
    half, count = depth // 2, ny * nx * tok
    any_spec, vmem = pl.BlockSpec(memory_space=pl.ANY), pl.BlockSpec(memory_space=pltpu.VMEM)
    sources = [first, *near, *left, *right]
    macs = count * depth * units * 6
    return pl.pallas_call(
        functools.partial(ffn_kernel, ny, nx, experts, per_group),
        in_specs=[any_spec] * len(sources) + [vmem] * 6,
        out_specs=[vmem] * 4,
        out_shape=[
            jax.ShapeDtypeStruct((ny - 1, nx * tok, half), jnp.bfloat16),
            jax.ShapeDtypeStruct((nx * tok, half), jnp.float32),
            jax.ShapeDtypeStruct((nx - 1, ny * tok, half), jnp.bfloat16),
            jax.ShapeDtypeStruct((ny * tok, half), jnp.float32),
        ],
        scratch_shapes=[
            pltpu.VMEM((count, width), jnp.bfloat16),
            pltpu.VMEM((2, count, units), jnp.bfloat16),
            pltpu.SemaphoreType.DMA((2 * ny * nx,)),
        ],
        compiler_params=pltpu.CompilerParams(vmem_limit_bytes=14 * 1024 * 1024),
        cost_estimate=pl.CostEstimate(
            flops=2 * macs,
            bytes_accessed=8 * count * depth,
            transcendentals=2 * count * units,
        ),
    )(*sources, *weights)


def shift(value, axis, by):
    n = lax.axis_size(axis)
    return lax.ppermute(value, axis, [(i, (i + by) % n) for i in range(n)])


def ring_step(value):
    n = lax.axis_size("line")
    order = list(range(1, n, 2)) + list(range(0, n, 2))[::-1]
    return lax.ppermute(value, "line", [(order[i], order[(i + 1) % n]) for i in range(n)])


def after(value, *earlier):
    return lax.optimization_barrier((value, earlier))[0]


def per_device(tokens, expert_ids, combine, gate_weight, up_weight, down_weight):
    ny, nx, stages = lax.axis_size("e_hi"), lax.axis_size("e_lo"), lax.axis_size("line")
    per_group, units, depth = gate_weight.shape
    experts = ny * nx * per_group
    tok = tokens.shape[0]
    half = depth // 2

    chosen = expert_ids[:, :, None] == jnp.arange(experts, dtype=jnp.int32)[None, None, :]
    named = jnp.sum(jnp.where(chosen, combine[:, :, None], 0.0), axis=1)
    high = named.astype(jnp.bfloat16)
    rest = (named - high.astype(jnp.float32)).astype(jnp.bfloat16)
    pad = jnp.zeros((tok, LANES * -(-2 * experts // LANES) - 2 * experts), jnp.bfloat16)
    first = jnp.concatenate([tokens, high, rest, pad], axis=1)

    def near_of(pieces):
        if nx == ny:
            lefts, rights = pieces[: nx - 1], pieces[nx - 1 :]
            return [jnp.concatenate([a, b], axis=1) for a, b in zip(lefts, rights)]
        return pieces

    def halves_of(near):
        if nx == ny:
            return [n[:, :half] for n in near], [n[:, half:] for n in near]
        return near[: nx - 1], near[nx - 1 :]

    near = [shift(tokens[:, :half], "e_lo", j) for j in range(1, nx)]
    near += [shift(first[:, half:], "e_hi", j) for j in range(1, ny)]
    near = near_of(near)

    own = [w.reshape(per_group * units, depth) for w in (gate_weight, up_weight, down_weight)]
    other = [shift(own[0], "core", 1)]

    def add(*terms):
        return sum(t.astype(jnp.float32) for t in terms)

    def exchange(first, near):
        lefts, rights = halves_of(near)
        left = jnp.concatenate([first[:, :half], *lefts])
        right = jnp.concatenate([first[:, half:], *rights])
        return (
            [shift(left, "e_hi", j) for j in range(1, ny)],
            [shift(right, "e_lo", j) for j in range(1, nx)],
        )

    def run(first, near, sides, *earlier):
        first, sides = after((first, sides), *earlier)
        if nx == ny:
            lefts, rights = halves_of(near)
            near = lefts + rights
        return ffn(first, near, *sides, weights, experts, per_group)

    def start_sums(parts, *earlier):
        send_a, keep_a, send_b, keep_b = parts
        send_a, send_b = after((send_a, send_b), *earlier)
        got_a = [shift(send_a[j - 1], "e_hi", -j) for j in range(1, ny)]
        got_b = [shift(send_b[j - 1], "e_lo", -j) for j in range(1, nx)]
        return [keep_a] + got_a, [keep_b] + got_b

    def finish_sums(terms_a, terms_b):
        sum_a = add(*terms_a).reshape(nx, tok, half)
        sum_b = add(*terms_b).reshape(ny, tok, half)
        last_a = [shift(sum_a[j].astype(jnp.bfloat16), "e_lo", -j) for j in range(1, nx)]
        last_b = [shift(sum_b[j].astype(jnp.bfloat16), "e_hi", -j) for j in range(1, ny)]
        return [sum_a[0]] + last_a, [sum_b[0]] + last_b

    firsts, nears, sides = [first], [near], [exchange(first, near)]
    firsts.append(ring_step(first))
    nears.append([ring_step(n) for n in near])
    other.append(shift(after(own[1], other[0], near, firsts[1]), "core", 1))
    other.append(shift(after(own[2], other[0], near, firsts[1]), "core", 1))
    weights = own + other

    parts, begun = {}, {}
    for k in range(1, stages):
        sides.append(exchange(firsts[k], nears[k]))
        if k + 1 < stages:
            if nx == ny:
                pair = jnp.concatenate([firsts[k], *nears[k]])
                pair = ring_step(pair)
                firsts.append(pair[:tok])
                nears.append([pair[i * tok : (i + 1) * tok] for i in range(1, nx)])
            else:
                firsts.append(ring_step(firsts[k]))
                nears.append([ring_step(n) for n in nears[k]])
        earlier = firsts[k], nears[k], begun.get(k - 2)
        parts[k - 1] = run(firsts[k - 1], nears[k - 1], sides[k - 1], *earlier)
        begun[k - 1] = start_sums(parts[k - 1], sides[k])
    last = stages - 1
    parts[last] = run(
        firsts[last], nears[last], sides[last], parts[last - 1], begun[last - 2]
    )
    begun[last] = start_sums(parts[last], begun[last - 1])

    carry_a, carry_b = [], []
    for k in list(range(1, stages)) + [0]:
        terms_a, terms_b = begun[k]
        if k == 1:
            sums = jnp.concatenate([add(*terms_a), add(*terms_b)], axis=1 if nx == ny else 0)
            sums = ring_step(sums.astype(jnp.bfloat16))
            if nx == ny:
                mid_a, mid_b = [sums[:, :half]], [sums[:, half:]]
            else:
                mid_a, mid_b = [sums[: nx * tok]], [sums[nx * tok :]]
            continue
        if k == 0:
            mid_a, mid_b = [], []
        a, b = finish_sums(terms_a + mid_a, terms_b + mid_b)
        mid_a, mid_b = [], []
        total = jnp.concatenate([add(*a, *carry_a), add(*b, *carry_b)], axis=1)
        total = total.astype(jnp.bfloat16)
        if k:
            total = ring_step(total)
            carry_a, carry_b = [total[:, :half]], [total[:, half:]]
    return total


def solution(mesh):
    groups, shards = mesh.shape["expert"], mesh.shape["fsdp"]
    split = Mesh(mesh.devices.reshape(groups // 2, 2, shards // 2, 2), AXES)
    whole, expert, shard = P(AXES, None), ("e_hi", "e_lo"), ("line", "core")
    return jax.shard_map(
        per_device,
        mesh=split,
        in_specs=(whole, whole, whole) + (P(expert, shard, None),) * 3,
        out_specs=whole,
        check_vma=False,
    )
```
